128 devices in a mesh: row: 32 (over z_lo, x, y), rep: 4 (over z_hi, core).
Axes of the slice: x: 4, y: 4, z: 4 (z_hi: 2, z_lo: 2; z = z_hi * 2 + z_lo), core: 2. Of those that a mesh axis runs over, the one named last changes fastest.
Arguments:
- features: bfloat16 [65536, 256], P(('row', 'rep')), may hold values from -6 to 6
- self_weight: bfloat16 [256, 256], replicated, may hold values from -0.375 to 0.375
- neigh_weight: bfloat16 [256, 256], replicated, may hold values from -0.375 to 0.375
- tile_rows: int32 [40960], P(('row', 'rep')), may hold values from 0 to 15, as said below
- tile_cols: int32 [40960], P(('row', 'rep')), may hold values from 0 to 511, as said below
- tile_masks: int32 [40960, 128, 128], P(('row', 'rep')), may hold values from 0 to 1, as said below
- cotangent: bfloat16 [65536, 256], P(('row', 'rep'))
Outputs:
- output: bfloat16 [65536, 256], P(('row', 'rep'))
- grad_features: bfloat16 [65536, 256], P(('row', 'rep'))
- grad_self_weight: float32 [256, 256], replicated
- grad_neigh_weight: float32 [256, 256], replicated
The draws below stay inside these ranges and needn't reach their ends.
Inputs may be any that keep to these rules, and one draw needn't show every extreme that they name: `tile_rows`: within one device's slots, a tile's block row inside that device's row block of 2048 nodes. `tile_cols`: on the device with rep index r, every slot's column c has (c // 4) % (number of rep devices) == r. Live tiles fill the first slots of a device, the rest are empty (zero masks); at most 320 tiles are live on a device and some device has all 320 live. `tile_masks`: every live tile has at least one nonzero; empty slots are all zero.
All inputs are finite; a program needn't handle non-finite values.
Results may differ from the reference program's by a relative error of at most 0.025.
Values may be sent and summed in bfloat16 or wider, within the bound.
No kernel may reach another device: no remote copies, remote signals or barrier semaphores. Data moves between devices by JAX's collectives and lax.ppermute only.
A program may use at most 192 MiB of HBM per device.

```python
import jax
import jax.numpy as jnp
from jax import lax

H = 256
TILE = 128
NODE_DEV = 512
TILES_DEV = 320
BLOCK_ROWS = 2048
NODES = 65536
ALL_TILES = 40960
N_ROW = 32
N_REP = 4


def tile_layout(key):
    devices = N_ROW * N_REP
    per_section = NODE_DEV // TILE
    per_block = NODE_DEV * N_REP // TILE
    k_live = jax.random.fold_in(key, 101)
    k_pick = jax.random.fold_in(key, 102)
    k_rows = jax.random.fold_in(key, 103)
    k_section = jax.random.fold_in(key, 104)
    k_local = jax.random.fold_in(key, 105)
    live = jax.random.randint(k_live, (devices,), TILES_DEV // 4, TILES_DEV + 1)
    picked = jax.random.randint(k_pick, (), 0, devices)
    live = jnp.where(jnp.arange(devices) == picked, TILES_DEV, live)
    slots = jnp.arange(TILES_DEV)
    alive = slots[None, :] < live[:, None]
    rows = jax.random.randint(k_rows, (devices, TILES_DEV), 0, per_block)
    section = jax.random.randint(k_section, (devices, TILES_DEV), 0, N_ROW)
    local = jax.random.randint(k_local, (devices, TILES_DEV), 0, per_section)
    rep_of = (jnp.arange(devices) % N_REP)[:, None]
    cols = (section * N_REP + rep_of) * per_section + local
    rows = jnp.where(alive, rows, 0)
    cols = jnp.where(alive, cols, rep_of * per_section)
    device_row = (jnp.arange(devices) // N_REP)[:, None]
    global_rows = device_row * per_block + rows
    return (alive.reshape(-1), rows.reshape(-1).astype(jnp.int32), cols.reshape(-1).astype(jnp.int32), global_rows.reshape(-1))


def draw_tile_rows(key, part):
    alive, rows, cols, global_rows = tile_layout(key)
    return rows


def draw_tile_cols(key, part):
    alive, rows, cols, global_rows = tile_layout(key)
    return cols


def draw_tile_masks(key, part):
    alive, rows, cols, global_rows = tile_layout(key)
    key = jax.random.fold_in(key, 7)
    k_rate = jax.random.fold_in(key, 1)
    k_bits = jax.random.fold_in(key, 2)
    rates = jax.random.randint(k_rate, (NODES,), 0, 9)
    node_of = global_rows[:, None] * TILE + jnp.arange(TILE)[None, :]
    entry_rate = rates[node_of]
    bits = jax.random.randint(k_bits, (ALL_TILES, TILE, TILE), 0, 64)
    masks = (bits < entry_rate[:, :, None]) & alive[:, None, None]
    masks = masks.at[:, 0, 0].set(alive)
    return masks.astype(jnp.int32)


def draw_cotangent(key, part):
    key = jax.random.fold_in(key, 11)
    k_first = jax.random.fold_in(key, 1)
    position = jnp.arange(NODES, dtype=jnp.float32) / NODES
    values = jax.random.normal(k_first, (NODES, H), jnp.float32) * (0.6 * 3.0 ** position)[:, None]
    return values.astype(jnp.bfloat16)


def block_levels(own_key, extent, cuts, least, high):
    loudness = 1.0
    for dim, blocks in cuts:
        steps = jax.random.uniform(jax.random.fold_in(jax.random.fold_in(own_key, 6), dim), (blocks,), jnp.float32, least / len(cuts), high / len(cuts))
        loudness = loudness * jnp.repeat(jnp.exp(steps), extent[dim] // blocks).reshape((-1,) + (1,) * (len(extent) - 1 - dim))
    return loudness


def bell_draw(own_key, dims, width, most, cuts=(), kind=jnp.bfloat16):
    drawn = jax.random.normal(own_key, dims, jnp.float32) * width
    if len(cuts) > 0:
        drawn = block_levels(own_key, dims, cuts, -0.22, 0.18) * drawn
    return jnp.clip(drawn, min=-most, max=most).astype(kind)


def setup_inputs(seed: int = 0) -> dict:
    key_of = jax.random.split(jax.random.key(seed), 8)
    return {
        "features": bell_draw(key_of[0], (NODES, H), 1.0, 6.0, ((0, 128),)),
        "self_weight": bell_draw(key_of[1], (H, H), H ** -0.5, 0.375),
        "neigh_weight": bell_draw(key_of[2], (H, H), H ** -0.5, 0.375),
        "tile_rows": draw_tile_rows(jax.random.fold_in(key_of[7], 71), 0),
        "tile_cols": draw_tile_cols(jax.random.fold_in(key_of[7], 71), 0),
        "tile_masks": draw_tile_masks(jax.random.fold_in(key_of[7], 71), 0),
        "cotangent": draw_cotangent(jax.random.fold_in(key_of[7], 71), 0),
    }


def reference(features, self_weight, neigh_weight, tile_rows, tile_cols, tile_masks, cotangent):
    ntiles = NODES // TILE
    blocks_per_row = BLOCK_ROWS // TILE
    per_section = NODE_DEV // TILE
    devices = N_ROW * N_REP
    group = 1024
    device_of = jnp.arange(ALL_TILES, dtype=jnp.int32) // TILES_DEV
    global_rows = device_of // N_REP * blocks_per_row + tile_rows
    nblocks = ALL_TILES // group
    masks_grouped = tile_masks.reshape(nblocks, group, TILE, TILE)
    rows_grouped = global_rows.astype(jnp.int32).reshape(nblocks, group)
    cols_grouped = tile_cols.astype(jnp.int32).reshape(nblocks, group)
    feat_tiles = features.astype(jnp.float32).reshape(ntiles, TILE, H)

    def forward_step(carry, item):
        summed, degree = carry
        masks, rows, cols = item
        mask_float = masks.astype(jnp.float32)
        prod = jnp.einsum('tij,tjh->tih', mask_float, feat_tiles[cols], precision=lax.Precision.HIGHEST)
        summed = summed.at[rows].add(prod)
        degree = degree.at[rows].add(lax.optimization_barrier(jnp.sum(mask_float, axis=2)))
        return ((summed, degree), None)
    init = (jnp.zeros((ntiles, TILE, H), jnp.float32), jnp.zeros((ntiles, TILE), jnp.float32))
    (summed, degree), _ = lax.scan(forward_step, init, (masks_grouped, rows_grouped, cols_grouped))
    summed = summed.reshape(NODES, H)
    degree = degree.reshape(NODES)
    scale = lax.rsqrt(jnp.maximum(degree, 1.0))
    agg = (summed * scale[:, None]).astype(jnp.bfloat16)
    pre = jnp.dot(features, self_weight, preferred_element_type=jnp.float32) + jnp.dot(agg, neigh_weight, preferred_element_type=jnp.float32)
    sig = jax.nn.sigmoid(pre)
    output = (pre * sig).astype(jnp.bfloat16)
    grad_pre = (cotangent.astype(jnp.float32) * sig * (1.0 + pre * (1.0 - sig))).astype(jnp.bfloat16)
    norm = NODES ** (-0.5)
    grad_self = jnp.dot(features.T, grad_pre, preferred_element_type=jnp.float32) * norm
    grad_neigh = jnp.dot(agg.T, grad_pre, preferred_element_type=jnp.float32) * norm
    grad_mean = (jnp.dot(grad_pre, neigh_weight.T, preferred_element_type=jnp.float32) * scale[:, None]).astype(jnp.bfloat16)
    grad_tiles = grad_mean.astype(jnp.float32).reshape(ntiles, TILE, H)
    masks_dev = tile_masks.reshape(devices, TILES_DEV, TILE, TILE)
    rows_dev = global_rows.astype(jnp.int32).reshape(devices, TILES_DEV)
    cols_dev = tile_cols.astype(jnp.int32).reshape(devices, TILES_DEV)
    reps = jnp.arange(devices, dtype=jnp.int32) % N_REP
    compact = jnp.arange(N_ROW * per_section, dtype=jnp.int32)

    def backward_step(carry, item):
        masks, rows, cols, rep_index = item
        mask_float = masks.astype(jnp.float32)
        prod = jnp.einsum('tij,tih->tjh', mask_float, grad_tiles[rows], precision=lax.Precision.HIGHEST)
        local_cols = cols // (per_section * N_REP) * per_section + cols % per_section
        partial_value = jnp.zeros((N_ROW * per_section, TILE, H), jnp.float32).at[local_cols].add(prod)
        rounded = lax.optimization_barrier(partial_value.astype(jnp.bfloat16)).astype(jnp.float32)
        targets = (compact // per_section * N_REP + rep_index) * per_section + compact % per_section
        return (carry.at[targets.astype(jnp.int32)].add(rounded), None)
    spread, _ = lax.scan(backward_step, jnp.zeros((ntiles, TILE, H), jnp.float32), (masks_dev, rows_dev, cols_dev, reps))
    grad_feat = (jnp.dot(grad_pre, self_weight.T, preferred_element_type=jnp.float32) + spread.reshape(NODES, H)).astype(jnp.bfloat16)
    return (output, grad_feat, grad_self, grad_neigh)
```

```python
import functools

import jax
import jax.numpy as jnp
from jax import lax
from jax.experimental import pallas as pl
from jax.experimental.pallas import tpu as pltpu
from jax.sharding import PartitionSpec as P

TILE = 128
GROUP = 8
CLASSES = 4
PIECES = 4
PIECE_BLOCKS = 8
CLASS_BLOCKS = PIECES * PIECE_BLOCKS
BLOCK_TILES = 16
BOTH = ("row", "rep")
MIB = 1024 * 1024


def pairs(step):
    out = []
    for z in range(2):
        for x in range(4):
            for y in range(4):
                for h in range(2):
                    for c in range(2):
                        src = (z * 16 + x * 4 + y) * 4 + h * 2 + c
                        z2, x2, y2, h2, c2 = step(z, x, y, h, c)
                        dst = ((z2 % 2) * 16 + (x2 % 4) * 4 + y2 % 4) * 4 + (h2 % 2) * 2 + c2 % 2
                        out.append((src, dst))
    return out


def move(value, step):
    return lax.ppermute(value, BOTH, pairs(step))


def swap_core(value):
    return move(value, lambda z, x, y, h, c: (z, x, y, h, c + 1))


def swap_high(value):
    return move(value, lambda z, x, y, h, c: (z, x, y, h + 1, c))


def swap_low(value):
    return move(value, lambda z, x, y, h, c: (z + 1, x, y, h, c))


def move_p(value, by):
    return move(value, lambda z, x, y, h, c: (z, x + by, y, h, c) if c == 0 else (z, x, y + by, h, c))


def move_q(value, by):
    return move(value, lambda z, x, y, h, c: (z, x, y + by, h, c) if c == 0 else (z, x + by, y, h, c))


def params(mib):
    return pltpu.CompilerParams(vmem_limit_bytes=mib * MIB)


def prep_kernel(rows_ref, mask_ref, plain_ref, turned_ref, degree_ref):
    step = pl.program_id(0)

    @pl.when(step == 0)
    def _():
        degree_ref[...] = jnp.zeros_like(degree_ref)

    for k in range(BLOCK_TILES):
        wide = mask_ref[k].astype(jnp.float32)
        plain_ref[k] = wide.astype(jnp.bfloat16)
        turned = wide.T
        turned_ref[k] = turned.astype(jnp.bfloat16)
        row = rows_ref[step * BLOCK_TILES + k]
        degree_ref[pl.ds(row, 1), :] += jnp.sum(turned, axis=0, keepdims=True)


def prep(tile_rows, tile_masks, block_count):
    slots = tile_masks.shape[0]
    block = pl.BlockSpec((BLOCK_TILES, TILE, TILE), lambda i: (i, 0, 0))
    return pl.pallas_call(
        prep_kernel,
        grid=(slots // BLOCK_TILES,),
        in_specs=[pl.BlockSpec(memory_space=pltpu.SMEM), block],
        out_specs=[block, block, pl.BlockSpec((block_count, TILE), lambda i: (0, 0))],
        out_shape=[
            jax.ShapeDtypeStruct((slots, TILE, TILE), jnp.bfloat16),
            jax.ShapeDtypeStruct((slots, TILE, TILE), jnp.bfloat16),
            jax.ShapeDtypeStruct((block_count, TILE), jnp.float32),
        ],
        compiler_params=params(16),
        cost_estimate=pl.CostEstimate(flops=0, bytes_accessed=slots * TILE * TILE * 8, transcendentals=0),
        name="prep",
    )(tile_rows, tile_masks)


def unpack(meta):
    return meta & 1023, (meta >> 10) & 31, meta >> 15


def each_group(first, last, meta_ref, masks_ref, buf, sems, body):
    def fetch(group):
        slot = lax.rem(group, 3)
        for u in range(GROUP):
            tile = unpack(meta_ref[group * GROUP + u])[0]
            pltpu.make_async_copy(masks_ref.at[tile], buf.at[slot, u], sems.at[slot]).start()

    for ahead in range(2):

        @pl.when(first + ahead < last)
        def _():
            fetch(first + ahead)

    def turn(group, carry):
        @pl.when(group + 2 < last)
        def _():
            fetch(group + 2)

        slot = lax.rem(group, 3)
        pltpu.make_async_copy(masks_ref.at[pl.ds(0, GROUP)], buf.at[slot], sems.at[slot]).wait()
        body(group, slot)
        return carry

    lax.fori_loop(first, last, turn, 0)


def forward_kernel(which, first_call, last_call, meta_ref, bounds_ref, masks_ref, *refs):
    pieces = refs[:PIECES]
    refs = refs[PIECES:]
    before = None
    if not first_call:
        before, refs = refs[0], refs[1:]
    if last_call:
        keep_ref, give_ref, feats, buf, sems, feat_sems, total = refs
    else:
        total, feats, buf, sems, feat_sems = refs
    rows = PIECE_BLOCKS * TILE
    copies = []
    for k, piece in enumerate(pieces):
        source = piece.at[0] if len(piece.shape) == 3 else piece
        copies.append(pltpu.make_async_copy(source, feats.at[pl.ds(k * rows, rows)], feat_sems.at[k]))
    if first_call:
        total[...] = jnp.zeros_like(total)
    else:
        copies.append(pltpu.make_async_copy(before, total, feat_sems.at[PIECES]))
    for copy in copies:
        copy.start()
    for copy in copies:
        copy.wait()

    def body(group, slot):
        for u in range(GROUP):
            _, row, block = unpack(meta_ref[group * GROUP + u])
            part = jnp.dot(
                buf[slot, u],
                feats[pl.ds(pl.multiple_of(block * TILE, TILE), TILE), :],
                preferred_element_type=jnp.float32,
            )
            total[pl.ds(pl.multiple_of(row * TILE, TILE), TILE), :] += part

    each_group(bounds_ref[which], bounds_ref[which + 1], meta_ref, masks_ref, buf, sems, body)
    if last_call:
        quarter = keep_ref.shape[1]
        core, high = bounds_ref[CLASSES + 1], bounds_ref[CLASSES + 2]
        for h in range(2):
            side = (high + h) % 2
            kept = pl.multiple_of((side * 2 + core) * quarter, quarter)
            given = pl.multiple_of((side * 2 + 1 - core) * quarter, quarter)
            keep_ref[h] = total[pl.ds(kept, quarter), :].astype(jnp.bfloat16)
            give_ref[h] = total[pl.ds(given, quarter), :].astype(jnp.bfloat16)


def forward_class(which, meta, bounds, masks, pieces, before, row_blocks):
    width = pieces[0].shape[-1]
    first_call, last_call = before is None, which == CLASSES - 1
    total_rows = (row_blocks + 1) * TILE
    feat_rows = (CLASS_BLOCKS + 1) * TILE
    scratch = [
        pltpu.VMEM((feat_rows, width), jnp.bfloat16),
        pltpu.VMEM((3, GROUP, TILE, TILE), jnp.bfloat16),
        pltpu.SemaphoreType.DMA((3,)),
        pltpu.SemaphoreType.DMA((PIECES + 1,)),
    ]
    vmem = pl.BlockSpec(memory_space=pltpu.VMEM)
    if last_call:
        half = jax.ShapeDtypeStruct((2, row_blocks * TILE // 4, width), jnp.bfloat16)
        out_shape, out_specs = [half, half], [vmem, vmem]
        scratch.append(pltpu.VMEM((total_rows, width), jnp.float32))
    else:
        out_shape, out_specs = jax.ShapeDtypeStruct((total_rows, width), jnp.float32), vmem
    smem = pl.BlockSpec(memory_space=pltpu.SMEM)
    anywhere = pl.BlockSpec(memory_space=pl.ANY)
    extra = [] if first_call else [before]
    tiles = masks.shape[0] // CLASSES
    return pl.pallas_call(
        functools.partial(forward_kernel, which, first_call, last_call),
        in_specs=[smem, smem] + [anywhere] * (1 + len(pieces) + len(extra)),
        out_specs=out_specs,
        out_shape=out_shape,
        scratch_shapes=scratch,
        compiler_params=params(16),
        cost_estimate=pl.CostEstimate(
            flops=tiles * TILE * TILE * width * 2 * 4, bytes_accessed=8 * MIB, transcendentals=0
        ),
        name=f"forward_class{which}",
    )(meta, bounds, masks, *pieces, *extra)


def backward_kernel(which, meta_ref, bounds_ref, masks_ref, own, far, near, cross, *refs):
    outs = refs[:PIECES]
    grads, buf, sems, grad_sems, total = refs[PIECES:]
    quarter = own.shape[0]
    core, high = bounds_ref[CLASSES + 1], bounds_ref[CLASSES + 2]
    copies = []
    for k, (piece, h, c) in enumerate(((own, 0, 0), (far, 1, 0), (near, 0, 1), (cross, 1, 1))):
        place = ((high + h) % 2) * 2 + (core + c) % 2
        target = grads.at[pl.ds(pl.multiple_of(place * quarter, quarter), quarter)]
        copies.append(pltpu.make_async_copy(piece, target, grad_sems.at[k]))
    for copy in copies:
        copy.start()
    total[...] = jnp.zeros_like(total)
    for copy in copies:
        copy.wait()

    def body(group, slot):
        for u in range(GROUP):
            _, row, block = unpack(meta_ref[group * GROUP + u])
            part = jnp.dot(
                buf[slot, u],
                grads[pl.ds(pl.multiple_of(row * TILE, TILE), TILE), :],
                preferred_element_type=jnp.float32,
            )
            total[pl.ds(pl.multiple_of(block * TILE, TILE), TILE), :] += part

    each_group(bounds_ref[which], bounds_ref[which + 1], meta_ref, masks_ref, buf, sems, body)
    rows = PIECE_BLOCKS * TILE
    for k, out in enumerate(outs):
        out[...] = total[k * rows : (k + 1) * rows, :].astype(jnp.bfloat16)


def backward_class(which, meta, bounds, masks, grads):
    quarter, width = grads[0].shape
    vmem = pl.BlockSpec(memory_space=pltpu.VMEM)
    smem = pl.BlockSpec(memory_space=pltpu.SMEM)
    anywhere = pl.BlockSpec(memory_space=pl.ANY)
    piece = jax.ShapeDtypeStruct((PIECE_BLOCKS * TILE, width), jnp.bfloat16)
    tiles = masks.shape[0] // CLASSES
    return pl.pallas_call(
        functools.partial(backward_kernel, which),
        in_specs=[smem, smem] + [anywhere] * 5,
        out_specs=[vmem] * PIECES,
        out_shape=[piece] * PIECES,
        scratch_shapes=[
            pltpu.VMEM((4 * quarter + TILE, width), jnp.bfloat16),
            pltpu.VMEM((3, GROUP, TILE, TILE), jnp.bfloat16),
            pltpu.SemaphoreType.DMA((3,)),
            pltpu.SemaphoreType.DMA((4,)),
            pltpu.VMEM(((CLASS_BLOCKS + 1) * TILE, width), jnp.float32),
        ],
        compiler_params=params(16),
        cost_estimate=pl.CostEstimate(
            flops=tiles * TILE * TILE * width * 2 * 4, bytes_accessed=8 * MIB, transcendentals=0
        ),
        name=f"backward_class{which}",
    )(meta, bounds, masks, *grads)


def dense_kernel(
    feat_ref, self_ref, neigh_ref, cot_ref, scale_ref, keep_ref, near_ref, far_ref,
    out_ref, back_ref, mean_ref, weight_ref,
):
    rows_first = (((0,), (0,)), ((), ()))
    cols_both = (((1,), (1,)), ((), ()))
    f32 = jnp.float32
    summed = keep_ref[0].astype(f32) + near_ref[0].astype(f32) + far_ref[...].astype(f32)
    scale = scale_ref[...]
    agg = (summed * scale).astype(jnp.bfloat16)
    feats = feat_ref[...]
    pre = jnp.dot(feats, self_ref[...], preferred_element_type=f32) + jnp.dot(
        agg, neigh_ref[...], preferred_element_type=f32
    )
    sig = jax.nn.sigmoid(pre)
    out_ref[...] = (pre * sig).astype(jnp.bfloat16)
    grad = (cot_ref[...].astype(f32) * sig * (1.0 + pre * (1.0 - sig))).astype(jnp.bfloat16)
    mean = lax.dot_general(grad, neigh_ref[...], cols_both, preferred_element_type=f32) * scale
    mean_ref[...] = mean.astype(jnp.bfloat16)
    width = feats.shape[1]
    weight_ref[:width, :] = lax.dot_general(feats, grad, rows_first, preferred_element_type=f32)
    weight_ref[width:, :] = lax.dot_general(agg, grad, rows_first, preferred_element_type=f32)
    back_ref[...] = lax.dot_general(grad, self_ref[...], cols_both, preferred_element_type=f32)


def dense(features, self_weight, neigh_weight, cotangent, scale, keep, near, far):
    rows, width = features.shape
    vmem = pl.BlockSpec(memory_space=pltpu.VMEM)
    return pl.pallas_call(
        dense_kernel,
        in_specs=[vmem] * 8,
        out_specs=[vmem] * 4,
        out_shape=[
            jax.ShapeDtypeStruct((rows, width), jnp.bfloat16),
            jax.ShapeDtypeStruct((rows, width), jnp.float32),
            jax.ShapeDtypeStruct((rows, width), jnp.bfloat16),
            jax.ShapeDtypeStruct((2 * width, width), jnp.float32),
        ],
        compiler_params=params(32),
        cost_estimate=pl.CostEstimate(
            flops=6 * 2 * rows * width * width, bytes_accessed=4 * MIB, transcendentals=rows * width
        ),
        name="dense",
    )(features, self_weight, neigh_weight, cotangent, scale, keep, near, far)


def plan_tiles(tile_rows, tile_cols, row_blocks):
    slots = tile_rows.shape[0]
    row_index, rep_index = lax.axis_index("row"), lax.axis_index("rep")
    z, x, y = row_index // 16, row_index // 4 % 4, row_index % 4
    core, high = rep_index % 2, rep_index // 2
    section, t = tile_cols // 16, tile_cols % 4
    stream = t // 2
    far_z = (section // 16 != z).astype(jnp.int32)
    dx, dy = (section // 4 % 4 - x) % 4, (section % 4 - y) % 4
    dp, dq = jnp.where(stream == 0, dx, dy), jnp.where(stream == 0, dy, dx)
    kind = jnp.where(dq == 0, 0, jnp.where(dq == 2, 3, 1 + far_z))
    pair = jnp.where(dq % 2 == 0, far_z, (dq == 1).astype(jnp.int32))
    piece = pair * 2 + (stream != core).astype(jnp.int32)
    place = jnp.where(dp == 0, 0, jnp.where(dp == 3, 1, jnp.where(dp == 1, 2, 3)))
    block = piece * PIECE_BLOCKS + place * 2 + t % 2
    slot = jnp.arange(slots, dtype=jnp.int32)
    code = slot + tile_rows * 1024 + block * 32768
    classes = jnp.arange(CLASSES, dtype=jnp.int32)
    counts = jnp.sum((kind[:, None] == classes[None, :]).astype(jnp.int32), axis=0)
    groups = (counts + GROUP - 1) // GROUP
    starts = jnp.sum(
        jnp.where(jnp.arange(CLASSES + 1)[:, None] > classes[None, :], groups[None, :], 0), axis=1
    )
    same_before = (kind[:, None] == kind[None, :]) & (slot[None, :] < slot[:, None])
    rank = jnp.sum(same_before.astype(jnp.int32), axis=1)
    start = jnp.sum(jnp.where(kind[:, None] == classes[None, :], starts[None, :CLASSES], 0), axis=1)
    position = start * GROUP + rank
    places = -(-(slots + CLASSES * (GROUP - 1)) // GROUP) * GROUP
    hit = jnp.arange(places, dtype=jnp.int32)[:, None] == position[None, :]
    pad = row_blocks * 1024 + CLASS_BLOCKS * 32768
    meta = pad + jnp.sum(jnp.where(hit, code[None, :] - pad, 0), axis=1)
    bounds = jnp.concatenate([starts, core[None], high[None]]).astype(jnp.int32)
    return meta.astype(jnp.int32), bounds, core, high


def gather(features, core):
    rows, width = features.shape
    half = rows // 2
    mine = lax.dynamic_slice_in_dim(features, core * half, half, 0)
    theirs = lax.dynamic_slice_in_dim(features, (1 - core) * half, half, 0)
    own = jnp.stack([mine, swap_core(theirs)])
    sides = []
    for start in (own, swap_low(own)):
        near = [start, move_p(start, 1), move_p(start, -1), move_p(start, 2)]
        block = jnp.stack(near, axis=1).reshape(2, 4 * half, width)
        below, above = move_q(block, 1), move_q(block, -1)
        sides.append((block, below, above, move_q(below[0], 1), move_q(above[1], -1)))
    classes = [[], [], [], []]
    for s, (block, below, above, far0, far1) in enumerate(sides):
        classes[0] += [block, swap_core(block[1])]
        classes[1 + s] += [below, swap_core(below[1]), above, swap_core(above[1])]
        classes[3] += [far0, swap_core(far1)]
    return classes


def add(*values):
    return sum(value.astype(jnp.float32) for value in values).astype(jnp.bfloat16)


def scatter(run_class, core):
    far = run_class(3)
    sides = [None, None]
    for s in (1, 0):
        from_below = move_q(far[2 * s], 1)
        from_above = move_q(swap_core(far[2 * s + 1]), -1)
        down, down_other, up, up_other = run_class(1 + s)
        to_above = jnp.stack([add(up, from_below), swap_core(up_other)])
        to_below = jnp.stack([down, add(swap_core(down_other), from_above)])
        sides[s] = (move_q(to_above, 1), move_q(to_below, -1))
    here = run_class(0)
    ends = [None, None]
    for s in (1, 0):
        total = add(jnp.stack([here[2 * s], swap_core(here[2 * s + 1])]), *sides[s])
        parts = total.reshape(2, 4, -1, total.shape[-1])
        ends[s] = sum(
            value.astype(jnp.float32)
            for value in (
                parts[:, 0],
                move_p(parts[:, 1], -1),
                move_p(parts[:, 2], 1),
                move_p(parts[:, 3], 2),
            )
        )
    end = ends[0] + swap_low(ends[1].astype(jnp.bfloat16)).astype(jnp.float32)
    mine = end[0]
    other = swap_core(end[1].astype(jnp.bfloat16)).astype(jnp.float32)
    first = jnp.where(core == 0, mine, other)
    second = jnp.where(core == 0, other, mine)
    return jnp.concatenate([first, second], axis=0)


def local(features, self_weight, neigh_weight, tile_rows, tile_cols, tile_masks, cotangent):
    rows, width = features.shape
    row_blocks = rows * 4 // TILE
    meta, bounds, core, high = plan_tiles(tile_rows, tile_cols, row_blocks)
    classes = gather(features, core)
    plain, turned, degree = prep(tile_rows, tile_masks, row_blocks)
    degree = degree + swap_core(degree)
    degree = degree + swap_high(degree)
    own_degree = lax.dynamic_slice_in_dim(
        degree, (high * 2 + core) * (row_blocks // 4), row_blocks // 4, 0
    )
    scale = jnp.broadcast_to(
        lax.rsqrt(jnp.maximum(own_degree, 1.0)).reshape(rows, 1), (rows, width)
    )
    total = None
    for which in range(CLASSES):
        total = forward_class(which, meta, bounds, plain, classes[which], total, row_blocks)
    keep, give = total
    near = swap_core(give)
    far = swap_high(add(keep[1], near[1]))
    output, back, mean, weight = dense(
        features, self_weight, neigh_weight, cotangent, scale, keep, near, far
    )
    weight = lax.psum(weight, BOTH) * ((rows * lax.axis_size(BOTH)) ** (-0.5))
    mean_far = swap_high(mean)
    grads = (mean, mean_far, swap_core(mean), swap_core(mean_far))
    incoming = scatter(
        lambda which: backward_class(which, meta, bounds, turned, grads), core
    )
    grad_feat = (back + incoming).astype(jnp.bfloat16)
    return (output, grad_feat, weight[:width], weight[width:])


def solution(mesh):
    in_specs = (
        P(BOTH, None),
        P(),
        P(),
        P(BOTH),
        P(BOTH),
        P(BOTH, None, None),
        P(BOTH, None),
    )
    out_specs = (P(BOTH, None), P(BOTH, None), P(), P())
    return jax.shard_map(local, mesh=mesh, in_specs=in_specs, out_specs=out_specs, check_vma=False)
```

```python
import functools

import jax
import jax.numpy as jnp
from jax import lax
from jax.experimental import pallas as pl
from jax.experimental.pallas import tpu as pltpu
from jax.sharding import PartitionSpec as P

TILE = 128
GROUP = 16
DEPTH = 4
CLASSES = 4
PIECES = 4
PIECE_BLOCKS = 8
CLASS_BLOCKS = PIECES * PIECE_BLOCKS
BLOCK_TILES = 16
BOTH = ("row", "rep")
MIB = 1024 * 1024


def pairs(step):
    out = []
    for z in range(2):
        for x in range(4):
            for y in range(4):
                for h in range(2):
                    for c in range(2):
                        src = (z * 16 + x * 4 + y) * 4 + h * 2 + c
                        z2, x2, y2, h2, c2 = step(z, x, y, h, c)
                        dst = ((z2 % 2) * 16 + (x2 % 4) * 4 + y2 % 4) * 4 + (h2 % 2) * 2 + c2 % 2
                        out.append((src, dst))
    return out


def move(value, step):
    return lax.ppermute(value, BOTH, pairs(step))


def swap_core(value):
    return move(value, lambda z, x, y, h, c: (z, x, y, h, c + 1))


def swap_high(value):
    return move(value, lambda z, x, y, h, c: (z, x, y, h + 1, c))


def swap_low(value):
    return move(value, lambda z, x, y, h, c: (z + 1, x, y, h, c))


def swap_x(value):
    return move(value, lambda z, x, y, h, c: (z, x ^ 1, y, h, c))


def swap_xx(value):
    return move(value, lambda z, x, y, h, c: (z, x + 2, y, h, c))


def swap_y(value):
    return move(value, lambda z, x, y, h, c: (z, x, y ^ 1, h, c))


def swap_yy(value):
    return move(value, lambda z, x, y, h, c: (z, x, y + 2, h, c))


def move_p(value, by):
    return move(value, lambda z, x, y, h, c: (z, x + by, y, h, c) if c == 0 else (z, x, y + by, h, c))


def move_q(value, by):
    return move(value, lambda z, x, y, h, c: (z, x, y + by, h, c) if c == 0 else (z, x + by, y, h, c))


def params(mib):
    return pltpu.CompilerParams(vmem_limit_bytes=mib * MIB)


def degree_kernel(rows_ref, mask_ref, tiles_ref, degree_ref, sums):
    step = pl.program_id(0)

    @pl.when(step == 0)
    def _():
        sums[...] = jnp.zeros_like(sums)

    for k in range(BLOCK_TILES):
        mask = mask_ref[k].astype(jnp.float32)
        row = rows_ref[step * BLOCK_TILES + k]
        sums[row] += mask
        tiles_ref[pl.ds(k, 1), :] = jnp.sum(mask, axis=0, keepdims=True)

    @pl.when(step == pl.num_programs(0) - 1)
    def _():
        for r in range(degree_ref.shape[0]):
            degree_ref[pl.ds(r, 1), :] = jnp.sum(sums[r].T, axis=0, keepdims=True)


def degrees(tile_rows, tile_masks, block_count):
    slots = tile_masks.shape[0]
    return pl.pallas_call(
        degree_kernel,
        grid=(slots // BLOCK_TILES,),
        in_specs=[
            pl.BlockSpec(memory_space=pltpu.SMEM),
            pl.BlockSpec((BLOCK_TILES, TILE, TILE), lambda i: (i, 0, 0)),
        ],
        out_specs=[
            pl.BlockSpec((BLOCK_TILES, TILE), lambda i: (i, 0)),
            pl.BlockSpec((block_count, TILE), lambda i: (0, 0)),
        ],
        out_shape=[
            jax.ShapeDtypeStruct((slots, TILE), jnp.float32),
            jax.ShapeDtypeStruct((block_count, TILE), jnp.float32),
        ],
        scratch_shapes=[pltpu.VMEM((block_count, TILE, TILE), jnp.float32)],
        compiler_params=params(48),
        cost_estimate=pl.CostEstimate(flops=0, bytes_accessed=slots * TILE * TILE * 4, transcendentals=0),
        name="degrees",
    )(tile_rows, tile_masks)


def unpack(meta):
    return meta & 1023, (meta >> 10) & 31, meta >> 15


def as_bf16(mask):
    return mask.astype(jnp.float32).astype(jnp.bfloat16)


def each_group(first, last, meta_ref, masks_ref, buf, sems, body):
    def fetch(group):
        slot = lax.rem(group, DEPTH)
        for u in range(GROUP):
            tile = unpack(meta_ref[group * GROUP + u])[0]
            pltpu.make_async_copy(masks_ref.at[tile], buf.at[slot, u], sems.at[slot]).start()

    for ahead in range(DEPTH - 1):

        @pl.when(first + ahead < last)
        def _():
            fetch(first + ahead)

    def turn(group, carry):
        @pl.when(group + DEPTH - 1 < last)
        def _():
            fetch(group + DEPTH - 1)

        slot = lax.rem(group, DEPTH)
        pltpu.make_async_copy(masks_ref.at[pl.ds(0, GROUP)], buf.at[slot], sems.at[slot]).wait()
        body(group, slot)
        return carry

    lax.fori_loop(first, last, turn, 0)


def forward_kernel(which, first_call, last_call, meta_ref, bounds_ref, masks_ref, *refs):
    pieces = refs[:PIECES]
    refs = refs[PIECES:]
    before = None
    if not first_call:
        before, refs = refs[0], refs[1:]
    if last_call:
        keep_ref, give_ref, feats, buf, sems, feat_sems, total = refs
    else:
        total, feats, buf, sems, feat_sems = refs
    rows = PIECE_BLOCKS * TILE
    copies = []
    for k, piece in enumerate(pieces):
        source = piece.at[0] if len(piece.shape) == 3 else piece
        copies.append(pltpu.make_async_copy(source, feats.at[pl.ds(k * rows, rows)], feat_sems.at[k]))
    if first_call:
        total[...] = jnp.zeros_like(total)
    else:
        copies.append(pltpu.make_async_copy(before, total, feat_sems.at[PIECES]))
    for copy in copies:
        copy.start()
    for copy in copies:
        copy.wait()

    def body(group, slot):
        for u in range(GROUP):
            _, row, block = unpack(meta_ref[group * GROUP + u])
            part = jnp.dot(
                as_bf16(buf[slot, u]),
                feats[pl.ds(pl.multiple_of(block * TILE, TILE), TILE), :],
                preferred_element_type=jnp.float32,
            )
            total[pl.ds(pl.multiple_of(row * TILE, TILE), TILE), :] += part

    each_group(bounds_ref[which], bounds_ref[which + 1], meta_ref, masks_ref, buf, sems, body)
    if last_call:
        quarter = keep_ref.shape[1]
        core, high = bounds_ref[CLASSES + 1], bounds_ref[CLASSES + 2]
        for h in range(2):
            side = (high + h) % 2
            kept = pl.multiple_of((side * 2 + core) * quarter, quarter)
            given = pl.multiple_of((side * 2 + 1 - core) * quarter, quarter)
            keep_ref[h] = total[pl.ds(kept, quarter), :].astype(jnp.bfloat16)
            give_ref[h] = total[pl.ds(given, quarter), :].astype(jnp.bfloat16)


def forward_class(which, meta, bounds, masks, pieces, before, row_blocks):
    width = pieces[0].shape[-1]
    first_call, last_call = before is None, which == CLASSES - 1
    total_rows = (row_blocks + 1) * TILE
    feat_rows = (CLASS_BLOCKS + 1) * TILE
    scratch = [
        pltpu.VMEM((feat_rows, width), jnp.bfloat16),
        pltpu.VMEM((DEPTH, GROUP, TILE, TILE), jnp.int32),
        pltpu.SemaphoreType.DMA((DEPTH,)),
        pltpu.SemaphoreType.DMA((PIECES + 1,)),
    ]
    vmem = pl.BlockSpec(memory_space=pltpu.VMEM)
    if last_call:
        half = jax.ShapeDtypeStruct((2, row_blocks * TILE // 4, width), jnp.bfloat16)
        out_shape, out_specs = [half, half], [vmem, vmem]
        scratch.append(pltpu.VMEM((total_rows, width), jnp.float32))
    else:
        out_shape, out_specs = jax.ShapeDtypeStruct((total_rows, width), jnp.float32), vmem
    smem = pl.BlockSpec(memory_space=pltpu.SMEM)
    anywhere = pl.BlockSpec(memory_space=pl.ANY)
    held = pl.BlockSpec(memory_space=pltpu.HBM)
    extra = [] if first_call else [before]
    tiles = masks.shape[0] // CLASSES
    return pl.pallas_call(
        functools.partial(forward_kernel, which, first_call, last_call),
        in_specs=[smem, smem, held] + [anywhere] * (len(pieces) + len(extra)),
        out_specs=out_specs,
        out_shape=out_shape,
        scratch_shapes=scratch,
        compiler_params=params(48),
        cost_estimate=pl.CostEstimate(
            flops=tiles * TILE * TILE * width * 2 * 4, bytes_accessed=8 * MIB, transcendentals=0
        ),
        name=f"forward_class{which}",
    )(meta, bounds, masks, *pieces, *extra)


def backward_kernel(which, meta_ref, bounds_ref, masks_ref, own, far, near, cross, *refs):
    outs = refs[:PIECES]
    grads, buf, sems, grad_sems, total = refs[PIECES:]
    quarter = own.shape[0]
    core, high = bounds_ref[CLASSES + 1], bounds_ref[CLASSES + 2]
    copies = []
    for k, (piece, h, c) in enumerate(((own, 0, 0), (far, 1, 0), (near, 0, 1), (cross, 1, 1))):
        place = ((high + h) % 2) * 2 + (core + c) % 2
        target = grads.at[pl.ds(pl.multiple_of(place * quarter, quarter), quarter)]
        copies.append(pltpu.make_async_copy(piece, target, grad_sems.at[k]))
    for copy in copies:
        copy.start()
    total[...] = jnp.zeros_like(total)
    for copy in copies:
        copy.wait()

    def body(group, slot):
        for u in range(GROUP):
            _, row, block = unpack(meta_ref[group * GROUP + u])
            part = lax.dot_general(
                as_bf16(buf[slot, u]),
                grads[pl.ds(pl.multiple_of(row * TILE, TILE), TILE), :],
                (((0,), (0,)), ((), ())),
                preferred_element_type=jnp.float32,
            )
            total[pl.ds(pl.multiple_of(block * TILE, TILE), TILE), :] += part

    each_group(bounds_ref[which], bounds_ref[which + 1], meta_ref, masks_ref, buf, sems, body)
    rows = PIECE_BLOCKS * TILE
    for k, out in enumerate(outs):
        out[...] = total[k * rows : (k + 1) * rows, :].astype(jnp.bfloat16)


def backward_class(which, meta, bounds, masks, grads):
    quarter, width = grads[0].shape
    vmem = pl.BlockSpec(memory_space=pltpu.VMEM)
    smem = pl.BlockSpec(memory_space=pltpu.SMEM)
    anywhere = pl.BlockSpec(memory_space=pl.ANY)
    held = pl.BlockSpec(memory_space=pltpu.HBM)
    piece = jax.ShapeDtypeStruct((PIECE_BLOCKS * TILE, width), jnp.bfloat16)
    tiles = masks.shape[0] // CLASSES
    return pl.pallas_call(
        functools.partial(backward_kernel, which),
        in_specs=[smem, smem, held] + [anywhere] * 4,
        out_specs=[vmem] * PIECES,
        out_shape=[piece] * PIECES,
        scratch_shapes=[
            pltpu.VMEM((4 * quarter + TILE, width), jnp.bfloat16),
            pltpu.VMEM((DEPTH, GROUP, TILE, TILE), jnp.int32),
            pltpu.SemaphoreType.DMA((DEPTH,)),
            pltpu.SemaphoreType.DMA((4,)),
            pltpu.VMEM(((CLASS_BLOCKS + 1) * TILE, width), jnp.float32),
        ],
        compiler_params=params(48),
        cost_estimate=pl.CostEstimate(
            flops=tiles * TILE * TILE * width * 2 * 4, bytes_accessed=8 * MIB, transcendentals=0
        ),
        name=f"backward_class{which}",
    )(meta, bounds, masks, *grads)


def dense_kernel(
    feat_ref, self_ref, neigh_ref, cot_ref, scale_ref, keep_ref, near_ref, far_ref,
    out_ref, back_ref, mean_ref, weight_ref,
):
    rows_first = (((0,), (0,)), ((), ()))
    cols_both = (((1,), (1,)), ((), ()))
    f32 = jnp.float32
    summed = keep_ref[0].astype(f32) + near_ref[0].astype(f32) + far_ref[...].astype(f32)
    scale = scale_ref[...]
    agg = (summed * scale).astype(jnp.bfloat16)
    feats = feat_ref[...]
    pre = jnp.dot(feats, self_ref[...], preferred_element_type=f32) + jnp.dot(
        agg, neigh_ref[...], preferred_element_type=f32
    )
    sig = jax.nn.sigmoid(pre)
    out_ref[...] = (pre * sig).astype(jnp.bfloat16)
    grad = (cot_ref[...].astype(f32) * sig * (1.0 + pre * (1.0 - sig))).astype(jnp.bfloat16)
    mean = lax.dot_general(grad, neigh_ref[...], cols_both, preferred_element_type=f32) * scale
    mean_ref[...] = mean.astype(jnp.bfloat16)
    width = feats.shape[1]
    weight_ref[:width, :] = lax.dot_general(feats, grad, rows_first, preferred_element_type=f32)
    weight_ref[width:, :] = lax.dot_general(agg, grad, rows_first, preferred_element_type=f32)
    back_ref[...] = lax.dot_general(grad, self_ref[...], cols_both, preferred_element_type=f32)


def dense(features, self_weight, neigh_weight, cotangent, scale, keep, near, far):
    rows, width = features.shape
    vmem = pl.BlockSpec(memory_space=pltpu.VMEM)
    return pl.pallas_call(
        dense_kernel,
        in_specs=[vmem] * 8,
        out_specs=[vmem] * 4,
        out_shape=[
            jax.ShapeDtypeStruct((rows, width), jnp.bfloat16),
            jax.ShapeDtypeStruct((rows, width), jnp.float32),
            jax.ShapeDtypeStruct((rows, width), jnp.bfloat16),
            jax.ShapeDtypeStruct((2 * width, width), jnp.float32),
        ],
        compiler_params=params(32),
        cost_estimate=pl.CostEstimate(
            flops=6 * 2 * rows * width * width, bytes_accessed=4 * MIB, transcendentals=rows * width
        ),
        name="dense",
    )(features, self_weight, neigh_weight, cotangent, scale, keep, near, far)


def plan_tiles(tile_rows, tile_cols, tile_sums, row_blocks):
    slots = tile_rows.shape[0]
    row_index, rep_index = lax.axis_index("row"), lax.axis_index("rep")
    z, x, y = row_index // 16, row_index // 4 % 4, row_index % 4
    core, high = rep_index % 2, rep_index // 2
    section, t = tile_cols // 16, tile_cols % 4
    stream = t // 2
    far_z = (section // 16 != z).astype(jnp.int32)
    dx, dy = (section // 4 % 4 - x) % 4, (section % 4 - y) % 4
    dp, dq = jnp.where(stream == 0, dx, dy), jnp.where(stream == 0, dy, dx)
    kind = jnp.where(dq == 0, 0, jnp.where(dq == 2, 3, 1 + far_z))
    kind = jnp.where(jnp.max(tile_sums, axis=1) > 0, kind, CLASSES)
    pair = jnp.where(dq % 2 == 0, far_z, (dq == 1).astype(jnp.int32))
    piece = pair * 2 + (stream != core).astype(jnp.int32)
    place = jnp.where(dp == 0, 0, jnp.where(dp == 3, 1, jnp.where(dp == 1, 2, 3)))
    block = piece * PIECE_BLOCKS + place * 2 + t % 2
    slot = jnp.arange(slots, dtype=jnp.int32)
    code = slot + tile_rows * 1024 + block * 32768
    classes = jnp.arange(CLASSES, dtype=jnp.int32)
    counts = jnp.sum((kind[:, None] == classes[None, :]).astype(jnp.int32), axis=0)
    groups = (counts + GROUP - 1) // GROUP
    starts = jnp.sum(
        jnp.where(jnp.arange(CLASSES + 1)[:, None] > classes[None, :], groups[None, :], 0), axis=1
    )
    same_before = (kind[:, None] == kind[None, :]) & (slot[None, :] < slot[:, None])
    rank = jnp.sum(same_before.astype(jnp.int32), axis=1)
    start = jnp.sum(jnp.where(kind[:, None] == classes[None, :], starts[None, :CLASSES], 0), axis=1)
    position = jnp.where(kind < CLASSES, start * GROUP + rank, -1)
    places = -(-(slots + CLASSES * (GROUP - 1)) // GROUP) * GROUP
    hit = jnp.arange(places, dtype=jnp.int32)[:, None] == position[None, :]
    pad = row_blocks * 1024 + CLASS_BLOCKS * 32768
    meta = pad + jnp.sum(jnp.where(hit, code[None, :] - pad, 0), axis=1)
    bounds = jnp.concatenate([starts, core[None], high[None]]).astype(jnp.int32)
    return meta.astype(jnp.int32), bounds


def tie(*values):
    return lax.optimization_barrier(values)


def add(*values):
    return sum(value.astype(jnp.float32) for value in values).astype(jnp.bfloat16)


def local(features, self_weight, neigh_weight, tile_rows, tile_cols, tile_masks, cotangent):
    rows, width = features.shape
    half = rows // 2
    row_blocks = rows * 4 // TILE
    core, high = lax.axis_index("rep") % 2, lax.axis_index("rep") // 2

    mine = lax.dynamic_slice_in_dim(features, core * half, half, 0)
    theirs = lax.dynamic_slice_in_dim(features, (1 - core) * half, half, 0)
    own = jnp.stack([mine, swap_core(theirs)])
    low = swap_low(own)
    near = [move_p(own, 1), move_p(own, -1), move_p(own, 2)]
    tile_sums, degree = degrees(tile_rows, tile_masks, row_blocks)
    *near, low, tile_sums, degree = tie(*near, low, tile_sums, degree)
    block0 = jnp.stack([own, *near], axis=1).reshape(2, 4 * half, width)
    below0, above0 = move_q(block0, 1), move_q(block0, -1)
    meta, bounds = plan_tiles(tile_rows, tile_cols, tile_sums, row_blocks)
    low, meta = tie(low, meta)
    near = [move_p(low, 1), move_p(low, -1), move_p(low, 2)]
    degree = degree + swap_core(degree)
    degree = degree + swap_high(degree)
    *near, degree = tie(*near, degree)
    block1 = jnp.stack([low, *near], axis=1).reshape(2, 4 * half, width)
    below1, above1 = move_q(block1, 1), move_q(block1, -1)

    def forward(which, before, *pieces):
        return forward_class(which, meta, bounds, tile_masks, pieces, before, row_blocks)

    own_degree = lax.dynamic_slice_in_dim(
        degree, (high * 2 + core) * (row_blocks // 4), row_blocks // 4, 0
    )
    scale = jnp.broadcast_to(
        lax.rsqrt(jnp.maximum(own_degree, 1.0)).reshape(rows, 1), (rows, width)
    )
    total = forward(0, None, block0, swap_core(block0[1]), block1, swap_core(block1[1]))
    below0, above0, total, scale = tie(below0, above0, total, scale)
    far00, far01 = move_q(below0[0], 1), move_q(above0[1], -1)
    total = forward(1, total, below0, swap_core(below0[1]), above0, swap_core(above0[1]))
    below1, above1, total = tie(below1, above1, total)
    far10, far11 = move_q(below1[0], 1), move_q(above1[1], -1)
    total = forward(2, total, below1, swap_core(below1[1]), above1, swap_core(above1[1]))
    keep, give = forward(3, total, far00, swap_core(far01), far10, swap_core(far11))

    near = swap_core(give)
    far = swap_high(add(keep[1], near[1]))
    output, back, mean, weight = dense(
        features, self_weight, neigh_weight, cotangent, scale, keep, near, far
    )
    mean_far = swap_high(mean)
    grads = (mean, mean_far, swap_core(mean), swap_core(mean_far))
    weight_mine = lax.dynamic_slice_in_dim(weight, core * width, width, 0)
    weight_theirs = lax.dynamic_slice_in_dim(weight, (1 - core) * width, width, 0)
    weight = weight_mine + swap_core(weight_theirs)

    def fold(weight, exchange):
        sent = weight.astype(jnp.bfloat16)
        return sent.astype(jnp.float32) + exchange(sent).astype(jnp.float32)

    def backward(which):
        return backward_class(which, meta, bounds, tile_masks, grads)

    far = backward(3)
    weight = fold(weight, swap_high)
    passed = {}
    for s in (1, 0):
        passed[s] = (move_q(far[2 * s], 1), move_q(swap_core(far[2 * s + 1]), -1))
    sides = {}
    for s, exchange in ((1, swap_low), (0, swap_x)):
        down, down_other, up, up_other = backward(1 + s)
        from_below, from_above = passed[s]
        down, down_other, up, up_other, from_below, from_above, weight = tie(
            down, down_other, up, up_other, from_below, from_above, weight
        )
        to_above = jnp.stack([add(up, from_below), swap_core(up_other)])
        to_below = jnp.stack([down, add(swap_core(down_other), from_above)])
        sides[s] = (move_q(to_above, 1), move_q(to_below, -1))
        weight = fold(weight, exchange)
    here = backward(0)
    *here, weight = tie(*here, weight)
    ends = {}
    for s, exchange in ((1, swap_xx), (0, swap_y)):
        from_below, from_above = sides[s]
        from_below, from_above, weight = tie(from_below, from_above, weight)
        total = add(jnp.stack([here[2 * s], swap_core(here[2 * s + 1])]), from_below, from_above)
        parts = total.reshape(2, 4, half, width)
        moved = (move_p(parts[:, 1], -1), move_p(parts[:, 2], 1), move_p(parts[:, 3], 2))
        weight = fold(weight, exchange)
        ends[s] = (parts[:, 0], *moved)
    passed = swap_low(add(*ends[1]))
    weight = fold(weight, swap_yy)
    end = sum(value.astype(jnp.float32) for value in (*ends[0], passed))
    other = swap_core(end[1].astype(jnp.bfloat16)).astype(jnp.float32)
    incoming = jnp.concatenate(
        [jnp.where(core == 0, end[0], other), jnp.where(core == 0, other, end[0])], axis=0
    )
    grad_feat = (back + incoming).astype(jnp.bfloat16)
    weight = weight * ((rows * lax.axis_size(BOTH)) ** (-0.5))
    weight_other = swap_core(weight)
    self_total = jnp.where(core == 0, weight, weight_other)
    neigh_total = jnp.where(core == 0, weight_other, weight)
    return (output, grad_feat, self_total, neigh_total)


def solution(mesh):
    in_specs = (
        P(BOTH, None),
        P(),
        P(),
        P(BOTH),
        P(BOTH),
        P(BOTH, None, None),
        P(BOTH, None),
    )
    out_specs = (P(BOTH, None), P(BOTH, None), P(), P())
    return jax.shard_map(local, mesh=mesh, in_specs=in_specs, out_specs=out_specs, check_vma=False)
```

```python
import functools

import jax
import jax.numpy as jnp
from jax import lax
from jax.experimental import pallas as pl
from jax.experimental.pallas import tpu as pltpu
from jax.sharding import PartitionSpec as P

TILE = 128
GROUP = 16
DEPTH = 4
CLASSES = 5
CLASS_BLOCKS = 32
BLOCK_TILES = 16
BOTH = ("row", "rep")
MIB = 1024 * 1024


def pairs(step):
    out = []
    for z in range(2):
        for x in range(4):
            for y in range(4):
                for h in range(2):
                    for c in range(2):
                        src = (z * 16 + x * 4 + y) * 4 + h * 2 + c
                        z2, x2, y2, h2, c2 = step(z, x, y, h, c)
                        dst = ((z2 % 2) * 16 + (x2 % 4) * 4 + y2 % 4) * 4 + (h2 % 2) * 2 + c2 % 2
                        out.append((src, dst))
    return out


def move(value, step):
    return lax.ppermute(value, BOTH, pairs(step))


def swap_core(value):
    return move(value, lambda z, x, y, h, c: (z, x, y, h, c + 1))


def swap_high(value):
    return move(value, lambda z, x, y, h, c: (z, x, y, h + 1, c))


def swap_low(value):
    return move(value, lambda z, x, y, h, c: (z + 1, x, y, h, c))


def swap_x(value):
    return move(value, lambda z, x, y, h, c: (z, x ^ 1, y, h, c))


def swap_xx(value):
    return move(value, lambda z, x, y, h, c: (z, x + 2, y, h, c))


def swap_y(value):
    return move(value, lambda z, x, y, h, c: (z, x, y ^ 1, h, c))


def swap_yy(value):
    return move(value, lambda z, x, y, h, c: (z, x, y + 2, h, c))


def move_p(value, by):
    return move(value, lambda z, x, y, h, c: (z, x + by, y, h, c) if c == 0 else (z, x, y + by, h, c))


def move_q(value, by):
    return move(value, lambda z, x, y, h, c: (z, x, y + by, h, c) if c == 0 else (z, x + by, y, h, c))


def params(mib):
    return pltpu.CompilerParams(vmem_limit_bytes=mib * MIB)


def degree_kernel(first, rows_ref, masks_ref, tiles_ref, degree_ref, sums, buf, sems):
    count = tiles_ref.shape[0] // BLOCK_TILES

    def fetch(group):
        source = masks_ref.at[pl.ds(first + group * BLOCK_TILES, BLOCK_TILES)]
        slot = lax.rem(group, DEPTH)
        return pltpu.make_async_copy(source, buf.at[slot], sems.at[slot])

    for group in range(DEPTH - 1):
        fetch(group).start()
    sums[...] = jnp.zeros_like(sums)

    def turn(group, carry):
        @pl.when(group + DEPTH - 1 < count)
        def _():
            fetch(group + DEPTH - 1).start()

        fetch(group).wait()
        slot = lax.rem(group, DEPTH)
        for k in range(BLOCK_TILES):
            mask = buf[slot, k].astype(jnp.float32)
            row = rows_ref[first + group * BLOCK_TILES + k]
            sums[row] += mask
            tiles_ref[pl.ds(group * BLOCK_TILES + k, 1), :] = jnp.sum(mask, axis=0, keepdims=True)
        return carry

    lax.fori_loop(0, count, turn, 0)
    for r in range(degree_ref.shape[0]):
        degree_ref[pl.ds(r, 1), :] = jnp.sum(sums[r].T, axis=0, keepdims=True)


def degrees(part, parts, tile_rows, tile_masks, block_count):
    slots = tile_masks.shape[0] // parts
    vmem = pl.BlockSpec(memory_space=pltpu.VMEM)
    return pl.pallas_call(
        functools.partial(degree_kernel, part * slots),
        in_specs=[pl.BlockSpec(memory_space=pltpu.SMEM), pl.BlockSpec(memory_space=pltpu.HBM)],
        out_specs=[vmem, vmem],
        out_shape=[
            jax.ShapeDtypeStruct((slots, TILE), jnp.float32),
            jax.ShapeDtypeStruct((block_count, TILE), jnp.float32),
        ],
        scratch_shapes=[
            pltpu.VMEM((block_count, TILE, TILE), jnp.float32),
            pltpu.VMEM((DEPTH, BLOCK_TILES, TILE, TILE), jnp.int32),
            pltpu.SemaphoreType.DMA((DEPTH,)),
        ],
        compiler_params=params(41),
        cost_estimate=pl.CostEstimate(flops=0, bytes_accessed=20 * MIB, transcendentals=0),
        name=f"degrees{part}",
    )(tile_rows, tile_masks)


def unpack(meta):
    return meta & 1023, (meta >> 10) & 31, meta >> 15


def as_bf16(mask):
    return mask.astype(jnp.float32).astype(jnp.bfloat16)


def each_group(first, last, meta_ref, masks_ref, buf, sems, body):
    def fetch(group):
        slot = lax.rem(group, DEPTH)
        for u in range(GROUP):
            tile = unpack(meta_ref[group * GROUP + u])[0]
            pltpu.make_async_copy(masks_ref.at[tile], buf.at[slot, u], sems.at[slot]).start()

    for ahead in range(DEPTH - 1):

        @pl.when(first + ahead < last)
        def _():
            fetch(first + ahead)

    def turn(group, carry):
        @pl.when(group + DEPTH - 1 < last)
        def _():
            fetch(group + DEPTH - 1)

        slot = lax.rem(group, DEPTH)
        pltpu.make_async_copy(masks_ref.at[pl.ds(0, GROUP)], buf.at[slot], sems.at[slot]).wait()
        body(group, slot)
        return carry

    lax.fori_loop(first, last, turn, 0)


def forward_kernel(begin, end, count, first_call, last_call, meta_ref, bounds_ref, masks_ref, *refs):
    pieces = refs[:count]
    refs = refs[count:]
    before = None
    if not first_call:
        before, refs = refs[0], refs[1:]
    if last_call:
        keep_ref, give_ref, feats, buf, sems, total = refs
    else:
        total, feats, buf, sems = refs
    start = 0
    for piece in pieces:
        feats[start : start + piece.shape[0], :] = piece[...]
        start += piece.shape[0]
    total[...] = jnp.zeros_like(total) if first_call else before[...]

    def body(group, slot):
        for u in range(GROUP):
            _, row, block = unpack(meta_ref[group * GROUP + u])
            part = jnp.dot(
                as_bf16(buf[slot, u]),
                feats[pl.ds(pl.multiple_of(block * TILE, TILE), TILE), :],
                preferred_element_type=jnp.float32,
            )
            total[pl.ds(pl.multiple_of(row * TILE, TILE), TILE), :] += part

    each_group(bounds_ref[begin], bounds_ref[end], meta_ref, masks_ref, buf, sems, body)
    if last_call:
        quarter = keep_ref.shape[1]
        core, high = bounds_ref[CLASSES + 1], bounds_ref[CLASSES + 2]
        for h in range(2):
            side = (high + h) % 2
            kept = pl.multiple_of((side * 2 + core) * quarter, quarter)
            given = pl.multiple_of((side * 2 + 1 - core) * quarter, quarter)
            keep_ref[h] = total[pl.ds(kept, quarter), :].astype(jnp.bfloat16)
            give_ref[h] = total[pl.ds(given, quarter), :].astype(jnp.bfloat16)


def forward_class(begin, end, meta, bounds, masks, pieces, before, row_blocks):
    width = pieces[0].shape[-1]
    first_call, last_call = before is None, end == CLASSES

    total_rows = (row_blocks + 1) * TILE
    feat_rows = (CLASS_BLOCKS + 1) * TILE
    scratch = [
        pltpu.VMEM((feat_rows, width), jnp.bfloat16),
        pltpu.VMEM((DEPTH, GROUP, TILE, TILE), jnp.int32),
        pltpu.SemaphoreType.DMA((DEPTH,)),
    ]
    vmem = pl.BlockSpec(memory_space=pltpu.VMEM)
    if last_call:
        half = jax.ShapeDtypeStruct((2, row_blocks * TILE // 4, width), jnp.bfloat16)
        out_shape, out_specs = [half, half], [vmem, vmem]
        scratch.append(pltpu.VMEM((total_rows, width), jnp.float32))
    else:
        out_shape, out_specs = jax.ShapeDtypeStruct((total_rows, width), jnp.float32), vmem
    smem = pl.BlockSpec(memory_space=pltpu.SMEM)
    held = pl.BlockSpec(memory_space=pltpu.HBM)
    extra = [] if first_call else [before]
    aliases = {} if first_call or last_call else {3 + len(pieces): 0}
    return pl.pallas_call(
        functools.partial(forward_kernel, begin, end, len(pieces), first_call, last_call),
        in_specs=[smem, smem, held] + [vmem] * (len(pieces) + len(extra)),
        out_specs=out_specs,
        out_shape=out_shape,
        scratch_shapes=scratch,
        input_output_aliases=aliases,
        compiler_params=params(41),
        cost_estimate=pl.CostEstimate(flops=0, bytes_accessed=16 * MIB, transcendentals=0),
        name=f"forward_class{begin}",
    )(meta, bounds, masks, *pieces, *extra)


def backward_kernel(which, count, meta_ref, bounds_ref, masks_ref, own, far, near, cross, *refs):
    extra, refs = (refs[0], refs[1:]) if which == 2 else (None, refs)
    outs = refs[:count]
    grads, buf, sems, total = refs[count:]
    quarter = own.shape[0]
    core, high = bounds_ref[CLASSES + 1], bounds_ref[CLASSES + 2]
    for piece, h, c in ((own, 0, 0), (far, 1, 0), (near, 0, 1), (cross, 1, 1)):
        place = ((high + h) % 2) * 2 + (core + c) % 2
        grads[pl.ds(pl.multiple_of(place * quarter, quarter), quarter), :] = piece[...]
    total[...] = jnp.zeros_like(total)

    def body(group, slot):
        for u in range(GROUP):
            _, row, block = unpack(meta_ref[group * GROUP + u])
            part = lax.dot_general(
                as_bf16(buf[slot, u]),
                grads[pl.ds(pl.multiple_of(row * TILE, TILE), TILE), :],
                (((0,), (0,)), ((), ())),
                preferred_element_type=jnp.float32,
            )
            total[pl.ds(pl.multiple_of(block * TILE, TILE), TILE), :] += part

    each_group(bounds_ref[which], bounds_ref[which + 1], meta_ref, masks_ref, buf, sems, body)
    start = 0
    for out in outs:
        size = out.shape[0] if extra is None else out.shape[0] - extra.shape[0]
        out[:size, :] = total[start : start + size, :].astype(jnp.bfloat16)
        start += size
        if extra is not None:
            out[size:, :] = extra[...]


def backward_class(which, meta, bounds, masks, grads, *extra):
    quarter, width = grads[0].shape
    vmem = pl.BlockSpec(memory_space=pltpu.VMEM)
    smem = pl.BlockSpec(memory_space=pltpu.SMEM)
    held = pl.BlockSpec(memory_space=pltpu.HBM)
    count = 2
    blocks = CLASS_BLOCKS // 2 if which in (2, 4) else CLASS_BLOCKS
    behind = sum(value.shape[0] for value in extra)
    piece = jax.ShapeDtypeStruct((blocks * TILE // count + behind, width), jnp.bfloat16)
    return pl.pallas_call(
        functools.partial(backward_kernel, which, count),
        in_specs=[smem, smem, held] + [vmem] * (4 + len(extra)),
        out_specs=[vmem] * count,
        out_shape=[piece] * count,
        scratch_shapes=[
            pltpu.VMEM((4 * quarter + TILE, width), jnp.bfloat16),
            pltpu.VMEM((DEPTH, GROUP, TILE, TILE), jnp.int32),
            pltpu.SemaphoreType.DMA((DEPTH,)),
            pltpu.VMEM(((CLASS_BLOCKS + 1) * TILE, width), jnp.float32),
        ],
        compiler_params=params(41),
        cost_estimate=pl.CostEstimate(flops=0, bytes_accessed=16 * MIB, transcendentals=0),
        name=f"backward_class{which}",
    )(meta, bounds, masks, *grads, *extra)


def dense_kernel(
    feat_hbm, self_hbm, neigh_hbm, cot_hbm, scale_ref, keep_ref, near_ref, far_ref,
    out_ref, back_ref, mean_ref, weight_ref,
    feat_ref, self_ref, neigh_ref, cot_ref, sems,
):
    rows_first = (((0,), (0,)), ((), ()))
    cols_both = (((1,), (1,)), ((), ()))
    f32 = jnp.float32
    pairs_in = (
        (feat_hbm, feat_ref), (self_hbm, self_ref), (neigh_hbm, neigh_ref), (cot_hbm, cot_ref)
    )
    copies = [pltpu.make_async_copy(a, b, sems.at[k]) for k, (a, b) in enumerate(pairs_in)]
    for copy in copies:
        copy.start()
    summed = keep_ref[0].astype(f32) + near_ref[0].astype(f32) + far_ref[...].astype(f32)
    scale = jnp.concatenate([scale_ref[...]] * (self_hbm.shape[1] // TILE), axis=1)
    agg = (summed * scale).astype(jnp.bfloat16)
    for copy in copies:
        copy.wait()
    feats = feat_ref[...]
    pre = jnp.dot(feats, self_ref[...], preferred_element_type=f32) + jnp.dot(
        agg, neigh_ref[...], preferred_element_type=f32
    )
    sig = jax.nn.sigmoid(pre)
    out_ref[...] = (pre * sig).astype(jnp.bfloat16)
    grad = (cot_ref[...].astype(f32) * sig * (1.0 + pre * (1.0 - sig))).astype(jnp.bfloat16)
    mean = lax.dot_general(grad, neigh_ref[...], cols_both, preferred_element_type=f32) * scale
    mean_ref[...] = mean.astype(jnp.bfloat16)
    width = feats.shape[1]
    weight_ref[:width, :] = lax.dot_general(feats, grad, rows_first, preferred_element_type=f32)
    weight_ref[width:, :] = lax.dot_general(agg, grad, rows_first, preferred_element_type=f32)
    back_ref[...] = lax.dot_general(grad, self_ref[...], cols_both, preferred_element_type=f32)


def dense(features, self_weight, neigh_weight, cotangent, scale, keep, near, far):
    rows, width = features.shape
    vmem = pl.BlockSpec(memory_space=pltpu.VMEM)
    return pl.pallas_call(
        dense_kernel,
        in_specs=[pl.BlockSpec(memory_space=pl.ANY)] * 4 + [vmem] * 4,
        out_specs=[vmem] * 4,
        scratch_shapes=[
            pltpu.VMEM((rows, width), jnp.bfloat16),
            pltpu.VMEM((width, width), jnp.bfloat16),
            pltpu.VMEM((width, width), jnp.bfloat16),
            pltpu.VMEM((rows, width), jnp.bfloat16),
            pltpu.SemaphoreType.DMA((4,)),
        ],
        out_shape=[
            jax.ShapeDtypeStruct((rows, width), jnp.bfloat16),
            jax.ShapeDtypeStruct((rows, width), jnp.float32),
            jax.ShapeDtypeStruct((rows, width), jnp.bfloat16),
            jax.ShapeDtypeStruct((2 * width, width), jnp.float32),
        ],
        compiler_params=params(56),
        cost_estimate=pl.CostEstimate(
            flops=6 * 2 * rows * width * width, bytes_accessed=4 * MIB, transcendentals=rows * width
        ),
        name="dense",
    )(features, self_weight, neigh_weight, cotangent, scale, keep, near, far)


def plan_tiles(tile_rows, tile_cols, tile_sums, row_blocks):
    slots = tile_rows.shape[0]
    row_index, rep_index = lax.axis_index("row"), lax.axis_index("rep")
    z, x, y = row_index // 16, row_index // 4 % 4, row_index % 4
    core, high = rep_index % 2, rep_index // 2
    section, t = tile_cols // 16, tile_cols % 4
    far_z = (section // 16 != z).astype(jnp.int32)
    dx, dy = (section // 4 % 4 - x) % 4, (section % 4 - y) % 4
    dp, dq = jnp.where(core == 0, dx, dy), jnp.where(core == 0, dy, dx)
    kind = jnp.where(dq == 0, 0, 2 * far_z + jnp.where(dq == 2, 2, 1))
    kind = jnp.where(jnp.max(tile_sums, axis=1) > 0, kind, CLASSES)
    piece = jnp.where(dq == 0, far_z, (dq == 1).astype(jnp.int32))
    place = jnp.where(dp == 0, 0, jnp.where(dp == 3, 1, jnp.where(dp == 1, 2, 3)))
    block = piece * 16 + place * 4 + t
    slot = jnp.arange(slots, dtype=jnp.int32)
    code = slot + tile_rows * 1024 + block * 32768
    classes = jnp.arange(CLASSES, dtype=jnp.int32)
    counts = jnp.sum((kind[:, None] == classes[None, :]).astype(jnp.int32), axis=0)
    groups = (counts + GROUP - 1) // GROUP
    starts = jnp.sum(
        jnp.where(jnp.arange(CLASSES + 1)[:, None] > classes[None, :], groups[None, :], 0), axis=1
    )
    same_before = (kind[:, None] == kind[None, :]) & (slot[None, :] < slot[:, None])
    rank = jnp.sum(same_before.astype(jnp.int32), axis=1)
    start = jnp.sum(jnp.where(kind[:, None] == classes[None, :], starts[None, :CLASSES], 0), axis=1)
    position = jnp.where(kind < CLASSES, start * GROUP + rank, -1)
    places = -(-(slots + CLASSES * (GROUP - 1)) // GROUP) * GROUP
    hit = jnp.arange(places, dtype=jnp.int32)[:, None] == position[None, :]
    pad = row_blocks * 1024 + CLASS_BLOCKS * 32768
    meta = pad + jnp.sum(jnp.where(hit, code[None, :] - pad, 0), axis=1)
    bounds = jnp.concatenate([starts, core[None], high[None]]).astype(jnp.int32)
    return meta.astype(jnp.int32), bounds


def tie(*values):
    return lax.optimization_barrier(values)


def add(*values):
    return sum(value.astype(jnp.float32) for value in values).astype(jnp.bfloat16)


def local(features, self_weight, neigh_weight, tile_rows, tile_cols, tile_masks, cotangent):
    rows, width = features.shape
    row_blocks = rows * 4 // TILE
    core, high = lax.axis_index("rep") % 2, lax.axis_index("rep") // 2

    low = swap_low(features)
    near = [move_p(features, 1), move_p(features, -1), move_p(features, 2)]
    sums0, degree0 = degrees(0, 2, tile_rows, tile_masks, row_blocks)
    *near, low, sums0, degree0 = tie(*near, low, sums0, degree0)
    block0 = jnp.concatenate([features, *near])
    block0, far, low, rows_after = tie(block0, near[2], low, tile_rows)
    below0, above0 = move_q(block0, 1), move_q(block0, -1)
    near = [move_p(low, 1), move_p(low, -1), swap_low(far)]
    sums1, degree1 = degrees(1, 2, rows_after, tile_masks, row_blocks)
    *near, sums1, degree1 = tie(*near, sums1, degree1)
    block1 = jnp.concatenate([low, *near])
    block1, sums1 = tie(block1, sums1)
    below1, above1 = move_q(block1, 1), move_q(block1, -1)
    meta, bounds = plan_tiles(
        tile_rows, tile_cols, jnp.concatenate([sums0, sums1]), row_blocks
    )
    degree = degree0 + degree1
    degree = degree + swap_core(degree)

    def forward(begin, end, before, *pieces):
        return forward_class(begin, end, meta, bounds, tile_masks, pieces, before, row_blocks)

    total = forward(0, 1, None, block0, block1)
    below0, above0, total = tie(below0, above0, total)
    edge = block0.shape[0] // 2
    start0, start1 = below0[:edge], above0[edge:]
    start0, start1, total = tie(start0, start1, total)
    far00, far01 = move_q(start0, 1), move_q(start1, -1)
    total = forward(1, 2, total, below0, above0)
    below1, above1, total = tie(below1, above1, total)
    start0, start1 = below1[:edge], above1[edge:]
    start0, start1, total = tie(start0, start1, total)
    far10, far11 = move_q(start0, 1), move_q(start1, -1)
    total = forward(3, 4, total, below1, above1)
    far00, far01, total = tie(far00, far01, total)
    total = forward(2, 3, total, far00, far01)
    far10, far11, total = tie(far10, far11, total)
    keep, give = forward(4, 5, total, far10, far11)
    degree = degree + swap_high(degree)
    own_degree = lax.dynamic_slice_in_dim(
        degree, (high * 2 + core) * (row_blocks // 4), row_blocks // 4, 0
    )
    scale = jnp.broadcast_to(
        lax.rsqrt(jnp.maximum(own_degree, 1.0)).reshape(rows, 1), (rows, TILE)
    )

    near = swap_core(give)
    far = swap_high(add(keep[1], near[1]))
    output, back, mean, weight = dense(
        features, self_weight, neigh_weight, cotangent, scale, keep, near, far
    )
    def fold(weight, exchange):
        sent = weight.astype(jnp.bfloat16)
        return sent.astype(jnp.float32) + exchange(sent).astype(jnp.float32)

    def ring_sum(own, below, above, across, odd):
        own, below, above, across = (v.astype(jnp.float32) for v in (own, below, above, across))
        beside, beyond = jnp.where(odd, below, above), jnp.where(odd, above, below)
        return ((own + beside) + (beyond + across)).astype(jnp.bfloat16)

    mean_far = swap_high(mean)
    mean_near = swap_core(mean)
    grads = (mean, mean_far, mean_near, swap_core(mean_far))
    weight_mine = lax.dynamic_slice_in_dim(weight, core * width, width, 0)
    weight_theirs = lax.dynamic_slice_in_dim(weight, (1 - core) * width, width, 0)
    weight = fold(fold(weight_mine + swap_core(weight_theirs), swap_low), swap_high)
    weight = weight.astype(jnp.bfloat16)
    row_index = lax.axis_index("row")
    odd_x, odd_y = row_index // 4 % 2 == 1, row_index % 2 == 1
    odd_p, odd_q = jnp.where(core == 0, odd_x, odd_y), jnp.where(core == 0, odd_y, odd_x)

    def backward(which, grads, *extra):
        return backward_class(which, meta, bounds, tile_masks, grads, *extra)

    far10, far11 = backward(4, grads)
    far10, far11, *grads = tie(far10, far11, *grads)
    below1, above1 = move_q(far10, 1), move_q(far11, -1)
    far00, far01 = backward(2, grads, weight)
    far00, far01, *grads = tie(far00, far01, *grads)
    below0, above0 = move_q(far00, 1), move_q(far01, -1)
    down, up = backward(3, grads)
    down, up, below1, above1 = tie(down, up, below1, above1)
    to_above = jnp.concatenate([add(up[:edge], below1), up[edge:]])
    to_below = jnp.concatenate([down[:edge], add(down[edge:], above1)])
    to_above, to_below, *grads = tie(to_above, to_below, *grads)
    from_below1, from_above1 = move_q(to_above, 1), move_q(to_below, -1)
    down, up = backward(1, grads)
    down, up, below0, above0 = tie(down, up, below0, above0)
    to_above = jnp.concatenate([add(up[:edge], below0[:edge]), up[edge:], below0[edge:]])
    to_below = jnp.concatenate([down[:edge], add(down[edge:], above0[:edge])])
    to_above, to_below, *grads = tie(to_above, to_below, *grads)
    from_below0, from_above0 = move_q(to_above, 1), move_q(to_below, -1)
    here0, here1 = backward(0, grads)
    here0, here1, from_below1, from_above1 = tie(here0, here1, from_below1, from_above1)
    total = add(here1, from_below1, from_above1)
    parts = [total[k * rows : (k + 1) * rows] for k in range(4)]
    moved = (move_p(parts[1], -1), move_p(parts[2], 1))
    low_far = swap_low(parts[3])
    own_part, *moved, low_far = tie(parts[0], *moved, low_far)
    low_own = swap_low(add(own_part, *moved))
    low_far, from_below0, from_above0 = tie(low_far, from_below0, from_above0)
    weight = ring_sum(weight, below0[edge:], above0[edge:], from_below0[2 * edge :], odd_q)
    total = add(here0[rows:], from_below0[rows : 2 * edge], from_above0[rows:])
    down = jnp.concatenate([total[:rows], weight])
    up = jnp.concatenate([total[rows : 2 * rows], weight])
    across = jnp.concatenate([add(total[2 * rows :], low_far), weight])
    from_above, from_below, from_across = move_p(down, -1), move_p(up, 1), move_p(across, 2)
    weight = ring_sum(weight, from_below[rows:], from_above[rows:], from_across[rows:], odd_p)
    weight = weight.astype(jnp.float32)
    incoming = sum(
        value[:rows].astype(jnp.float32)
        for value in (here0, from_below0, from_above0, low_own, from_above, from_below, from_across)
    )
    grad_feat = (back + incoming).astype(jnp.bfloat16)
    weight = weight * ((rows * lax.axis_size(BOTH)) ** (-0.5))
    weight_other = swap_core(weight)
    self_total = jnp.where(core == 0, weight, weight_other)
    neigh_total = jnp.where(core == 0, weight_other, weight)
    return (output, grad_feat, self_total, neigh_total)


def solution(mesh):
    in_specs = (
        P(BOTH, None),
        P(),
        P(),
        P(BOTH),
        P(BOTH),
        P(BOTH, None, None),
        P(BOTH, None),
    )
    out_specs = (P(BOTH, None), P(BOTH, None), P(), P())
    return jax.shard_map(local, mesh=mesh, in_specs=in_specs, out_specs=out_specs, check_vma=False)
```

```python
import functools

import jax
import jax.numpy as jnp
from jax import lax
from jax.experimental import pallas as pl
from jax.experimental.pallas import tpu as pltpu
from jax.sharding import PartitionSpec as P

TILE = 128
GROUP = 16
DEPTH = 4
CLASSES = 5
CLASS_BLOCKS = 32
BLOCK_TILES = 16
BOTH = ("row", "rep")
MIB = 1024 * 1024


def pairs(step):
    out = []
    for z in range(2):
        for x in range(4):
            for y in range(4):
                for h in range(2):
                    for c in range(2):
                        src = (z * 16 + x * 4 + y) * 4 + h * 2 + c
                        z2, x2, y2, h2, c2 = step(z, x, y, h, c)
                        dst = ((z2 % 2) * 16 + (x2 % 4) * 4 + y2 % 4) * 4 + (h2 % 2) * 2 + c2 % 2
                        out.append((src, dst))
    return out


def move(value, step):
    return lax.ppermute(value, BOTH, pairs(step))


def swap_core(value):
    return move(value, lambda z, x, y, h, c: (z, x, y, h, c + 1))


def swap_high(value):
    return move(value, lambda z, x, y, h, c: (z, x, y, h + 1, c))


def swap_low(value):
    return move(value, lambda z, x, y, h, c: (z + 1, x, y, h, c))


def move_p(value, by):
    return move(value, lambda z, x, y, h, c: (z, x + by, y, h, c) if c == 0 else (z, x, y + by, h, c))


def move_q(value, by):
    return move(value, lambda z, x, y, h, c: (z, x, y + by, h, c) if c == 0 else (z, x + by, y, h, c))


def params(mib):
    return pltpu.CompilerParams(vmem_limit_bytes=mib * MIB)


def degree_kernel(first, rows_ref, masks_ref, tiles_ref, degree_ref, sums, buf, sems):
    count = tiles_ref.shape[0] // BLOCK_TILES

    def fetch(group):
        source = masks_ref.at[pl.ds(first + group * BLOCK_TILES, BLOCK_TILES)]
        slot = lax.rem(group, DEPTH)
        return pltpu.make_async_copy(source, buf.at[slot], sems.at[slot])

    for group in range(DEPTH - 1):
        fetch(group).start()
    sums[...] = jnp.zeros_like(sums)

    def turn(group, carry):
        @pl.when(group + DEPTH - 1 < count)
        def _():
            fetch(group + DEPTH - 1).start()

        fetch(group).wait()
        slot = lax.rem(group, DEPTH)
        for k in range(BLOCK_TILES):
            mask = buf[slot, k].astype(jnp.float32)
            row = rows_ref[first + group * BLOCK_TILES + k]
            sums[row] += mask
            tiles_ref[pl.ds(group * BLOCK_TILES + k, 1), :] = jnp.sum(mask, axis=0, keepdims=True)
        return carry

    lax.fori_loop(0, count, turn, 0)
    for r in range(degree_ref.shape[0]):
        degree_ref[pl.ds(r, 1), :] = jnp.sum(sums[r].T, axis=0, keepdims=True)


def degrees(part, parts, tile_rows, tile_masks, block_count):
    slots = tile_masks.shape[0] // parts
    vmem = pl.BlockSpec(memory_space=pltpu.VMEM)
    return pl.pallas_call(
        functools.partial(degree_kernel, part * slots),
        in_specs=[pl.BlockSpec(memory_space=pltpu.SMEM), pl.BlockSpec(memory_space=pltpu.HBM)],
        out_specs=[vmem, vmem],
        out_shape=[
            jax.ShapeDtypeStruct((slots, TILE), jnp.float32),
            jax.ShapeDtypeStruct((block_count, TILE), jnp.float32),
        ],
        scratch_shapes=[
            pltpu.VMEM((block_count, TILE, TILE), jnp.float32),
            pltpu.VMEM((DEPTH, BLOCK_TILES, TILE, TILE), jnp.int32),
            pltpu.SemaphoreType.DMA((DEPTH,)),
        ],
        compiler_params=params(41),
        cost_estimate=pl.CostEstimate(flops=0, bytes_accessed=20 * MIB, transcendentals=0),
        name=f"degrees{part}",
    )(tile_rows, tile_masks)


def unpack(meta):
    return meta & 1023, (meta >> 10) & 31, meta >> 15


def as_bf16(mask):
    return mask.astype(jnp.float32).astype(jnp.bfloat16)


def fetch_tiles(group, meta_ref, masks_ref, buf, sems):
    slot = lax.rem(group, DEPTH)
    for u in range(GROUP):
        tile = unpack(meta_ref[group * GROUP + u])[0]
        pltpu.make_async_copy(masks_ref.at[tile], buf.at[slot, u], sems.at[slot]).start()


def first_groups(first, last, *fetch_args):
    for ahead in range(DEPTH - 1):

        @pl.when(first + ahead < last)
        def _():
            fetch_tiles(first + ahead, *fetch_args)


def each_group(first, last, meta_ref, masks_ref, buf, sems, body):
    def turn(group, carry):
        @pl.when(group + DEPTH - 1 < last)
        def _():
            fetch_tiles(group + DEPTH - 1, meta_ref, masks_ref, buf, sems)

        slot = lax.rem(group, DEPTH)
        pltpu.make_async_copy(masks_ref.at[pl.ds(0, GROUP)], buf.at[slot], sems.at[slot]).wait()
        body(group, slot)
        return carry

    lax.fori_loop(first, last, turn, 0)


def forward_kernel(begin, end, count, first_call, last_call, meta_ref, bounds_ref, masks_ref, *refs):
    pieces = refs[:count]
    refs = refs[count:]
    before = None
    if not first_call:
        before, refs = refs[0], refs[1:]
    if last_call:
        keep_ref, give_ref, feats, buf, sems, total = refs
    else:
        total, feats, buf, sems = refs
    first, last = bounds_ref[begin], bounds_ref[end]
    first_groups(first, last, meta_ref, masks_ref, buf, sems)
    start = 0
    for piece in pieces:
        feats[start : start + piece.shape[0], :] = piece[...]
        start += piece.shape[0]
    total[...] = jnp.zeros_like(total) if first_call else before[...]

    def body(group, slot):
        for u in range(GROUP):
            _, row, block = unpack(meta_ref[group * GROUP + u])
            part = jnp.dot(
                as_bf16(buf[slot, u]),
                feats[pl.ds(pl.multiple_of(block * TILE, TILE), TILE), :],
                preferred_element_type=jnp.float32,
            )
            total[pl.ds(pl.multiple_of(row * TILE, TILE), TILE), :] += part

    each_group(first, last, meta_ref, masks_ref, buf, sems, body)
    if last_call:
        quarter = keep_ref.shape[1]
        core, high = bounds_ref[CLASSES + 1], bounds_ref[CLASSES + 2]
        for h in range(2):
            side = (high + h) % 2
            kept = pl.multiple_of((side * 2 + core) * quarter, quarter)
            given = pl.multiple_of((side * 2 + 1 - core) * quarter, quarter)
            keep_ref[h] = total[pl.ds(kept, quarter), :].astype(jnp.bfloat16)
            give_ref[h] = total[pl.ds(given, quarter), :].astype(jnp.bfloat16)


def forward_class(begin, end, meta, bounds, masks, pieces, before, row_blocks):
    width = pieces[0].shape[-1]
    first_call, last_call = before is None, end == CLASSES

    total_rows = (row_blocks + 1) * TILE
    feat_rows = (CLASS_BLOCKS + 1) * TILE
    scratch = [
        pltpu.VMEM((feat_rows, width), jnp.bfloat16),
        pltpu.VMEM((DEPTH, GROUP, TILE, TILE), jnp.int32),
        pltpu.SemaphoreType.DMA((DEPTH,)),
    ]
    vmem = pl.BlockSpec(memory_space=pltpu.VMEM)
    if last_call:
        half = jax.ShapeDtypeStruct((2, row_blocks * TILE // 4, width), jnp.bfloat16)
        out_shape, out_specs = [half, half], [vmem, vmem]
        scratch.append(pltpu.VMEM((total_rows, width), jnp.float32))
    else:
        out_shape, out_specs = jax.ShapeDtypeStruct((total_rows, width), jnp.float32), vmem
    smem = pl.BlockSpec(memory_space=pltpu.SMEM)
    held = pl.BlockSpec(memory_space=pltpu.HBM)
    extra = [] if first_call else [before]
    aliases = {} if first_call or last_call else {3 + len(pieces): 0}
    return pl.pallas_call(
        functools.partial(forward_kernel, begin, end, len(pieces), first_call, last_call),
        in_specs=[smem, smem, held] + [vmem] * (len(pieces) + len(extra)),
        out_specs=out_specs,
        out_shape=out_shape,
        scratch_shapes=scratch,
        input_output_aliases=aliases,
        compiler_params=params(41),
        cost_estimate=pl.CostEstimate(flops=0, bytes_accessed=16 * MIB, transcendentals=0),
        name=f"forward_class{begin}",
    )(meta, bounds, masks, *pieces, *extra)


def backward_kernel(which, count, meta_ref, bounds_ref, masks_ref, own, far, near, cross, *refs):
    arrived, refs = (refs[:2], refs[2:]) if which % 2 else (None, refs)
    outs, refs = refs[:count], refs[count:]
    if which == 1:
        passed, refs = refs[0], refs[1:]
    grads, buf, sems, total = refs
    quarter = own.shape[0]
    core, high = bounds_ref[CLASSES + 1], bounds_ref[CLASSES + 2]
    first, last = bounds_ref[which], bounds_ref[which + 1]
    first_groups(first, last, meta_ref, masks_ref, buf, sems)
    for piece, h, c in ((own, 0, 0), (far, 1, 0), (near, 0, 1), (cross, 1, 1)):
        place = ((high + h) % 2) * 2 + (core + c) % 2
        grads[pl.ds(pl.multiple_of(place * quarter, quarter), quarter), :] = piece[...]
    if arrived is None:
        total[...] = jnp.zeros_like(total)
    else:
        below, above = arrived
        edge = CLASS_BLOCKS * TILE // 4
        total[:edge, :] = jnp.zeros((edge, total.shape[1]), jnp.float32)
        total[edge : 2 * edge, :] = above[:edge, :].astype(jnp.float32)
        total[2 * edge : 3 * edge, :] = below[:edge, :].astype(jnp.float32)
        total[3 * edge :, :] = jnp.zeros((edge + TILE, total.shape[1]), jnp.float32)

    def body(group, slot):
        for u in range(GROUP):
            _, row, block = unpack(meta_ref[group * GROUP + u])
            part = lax.dot_general(
                as_bf16(buf[slot, u]),
                grads[pl.ds(pl.multiple_of(row * TILE, TILE), TILE), :],
                (((0,), (0,)), ((), ())),
                preferred_element_type=jnp.float32,
            )
            total[pl.ds(pl.multiple_of(block * TILE, TILE), TILE), :] += part

    each_group(first, last, meta_ref, masks_ref, buf, sems, body)
    size = CLASS_BLOCKS * TILE // (2 if which in (0, 1, 3) else 4)
    for k, out in enumerate(outs):
        out[:size, :] = total[k * size : (k + 1) * size, :].astype(jnp.bfloat16)
    if which == 1:
        behind = below.shape[0] - edge
        outs[1][size:, :] = below[edge:, :]
        passed[:behind, :] = below[edge:, :]
        passed[behind:, :] = above[edge:, :]


def backward_class(which, meta, bounds, masks, grads, *arrived):
    quarter, width = grads[0].shape
    vmem = pl.BlockSpec(memory_space=pltpu.VMEM)
    smem = pl.BlockSpec(memory_space=pltpu.SMEM)
    held = pl.BlockSpec(memory_space=pltpu.HBM)
    count = 2
    blocks = CLASS_BLOCKS // 2 if which in (2, 4) else CLASS_BLOCKS
    sizes = [blocks * TILE // count] * count
    if which == 1:
        behind = arrived[0].shape[0] - sizes[0] // 2
        sizes = [sizes[0], sizes[1] + behind, 2 * behind]
    return pl.pallas_call(
        functools.partial(backward_kernel, which, count),
        in_specs=[smem, smem, held] + [vmem] * (4 + len(arrived)),
        out_specs=[vmem] * len(sizes),
        out_shape=[jax.ShapeDtypeStruct((size, width), jnp.bfloat16) for size in sizes],
        scratch_shapes=[
            pltpu.VMEM((4 * quarter + TILE, width), jnp.bfloat16),
            pltpu.VMEM((DEPTH, GROUP, TILE, TILE), jnp.int32),
            pltpu.SemaphoreType.DMA((DEPTH,)),
            pltpu.VMEM(((CLASS_BLOCKS + 1) * TILE, width), jnp.float32),
        ],
        compiler_params=params(41),
        cost_estimate=pl.CostEstimate(flops=0, bytes_accessed=16 * MIB, transcendentals=0),
        name=f"backward_class{which}",
    )(meta, bounds, masks, *grads, *arrived)


def before_kernel(feat_ref, self_ref, neigh_ref, cot_ref, keep_ref, pre_ref, neigh_out, cot_out, sum_ref):
    pre_ref[...] = jnp.dot(feat_ref[...], self_ref[...], preferred_element_type=jnp.float32)
    neigh_out[...] = neigh_ref[...]
    cot_out[...] = cot_ref[...]
    sum_ref[...] = keep_ref[0]


def before_dense(features, self_weight, neigh_weight, cotangent, keep):
    rows, width = features.shape
    vmem = pl.BlockSpec(memory_space=pltpu.VMEM)
    return pl.pallas_call(
        before_kernel,
        in_specs=[vmem] * 5,
        out_specs=[vmem] * 4,
        out_shape=[
            jax.ShapeDtypeStruct((rows, width), jnp.float32),
            jax.ShapeDtypeStruct((width, width), jnp.bfloat16),
            jax.ShapeDtypeStruct((rows, width), jnp.bfloat16),
            jax.ShapeDtypeStruct((rows, width), jnp.bfloat16),
        ],
        compiler_params=params(32),
        cost_estimate=pl.CostEstimate(
            flops=2 * rows * width * width, bytes_accessed=2 * MIB, transcendentals=0
        ),
        name="before_dense",
    )(features, self_weight, neigh_weight, cotangent, keep)


def dense_kernel(
    pre_ref, neigh_ref, cot_ref, degree_ref, keep_ref, near_ref, far_ref,
    mean_ref, grad_ref, agg_ref, out_ref,
):
    cols_both = (((1,), (1,)), ((), ()))
    f32 = jnp.float32
    inverse = lax.rsqrt(jnp.maximum(degree_ref[...], 1.0))
    width = pre_ref.shape[1]
    columns = [
        jnp.broadcast_to(inverse[r : r + 1, :], (TILE, TILE)).T for r in range(inverse.shape[0])
    ]
    scale = jnp.concatenate([jnp.concatenate(columns, axis=0)] * (width // TILE), axis=1)
    summed = keep_ref[...].astype(f32) + near_ref[0].astype(f32) + far_ref[...].astype(f32)
    agg = (summed * scale).astype(jnp.bfloat16)
    pre = pre_ref[...] + jnp.dot(agg, neigh_ref[...], preferred_element_type=f32)
    sig = jax.nn.sigmoid(pre)
    out_ref[...] = (pre * sig).astype(jnp.bfloat16)
    grad = (cot_ref[...].astype(f32) * sig * (1.0 + pre * (1.0 - sig))).astype(jnp.bfloat16)
    mean = lax.dot_general(grad, neigh_ref[...], cols_both, preferred_element_type=f32) * scale
    mean_ref[...] = mean.astype(jnp.bfloat16)
    grad_ref[...] = grad
    agg_ref[...] = agg


def dense(pre, neigh_weight, cotangent, degree, keep, near, far):
    rows, width = pre.shape
    vmem = pl.BlockSpec(memory_space=pltpu.VMEM)
    return pl.pallas_call(
        dense_kernel,
        in_specs=[vmem] * 7,
        out_specs=[vmem] * 4,
        out_shape=[jax.ShapeDtypeStruct((rows, width), jnp.bfloat16)] * 4,
        compiler_params=params(32),
        cost_estimate=pl.CostEstimate(
            flops=2 * 2 * rows * width * width, bytes_accessed=4 * MIB, transcendentals=rows * width
        ),
        name="dense",
    )(pre, neigh_weight, cotangent, degree, keep, near, far)


def weights_kernel(core_ref, feat_ref, agg_ref, grad_ref, mine_ref, theirs_ref):
    rows_first = (((0,), (0,)), ((), ()))
    f32 = jnp.float32
    grad = grad_ref[...]
    parts = [
        lax.dot_general(value[...], grad, rows_first, preferred_element_type=f32)
        for value in (feat_ref, agg_ref)
    ]
    on_first = core_ref[0] == 0
    mine_ref[...] = jnp.where(on_first, parts[0], parts[1])
    theirs_ref[...] = jnp.where(on_first, parts[1], parts[0])


def weight_parts(core, features, agg, grad):
    rows, width = features.shape
    vmem = pl.BlockSpec(memory_space=pltpu.VMEM)
    return pl.pallas_call(
        weights_kernel,
        in_specs=[pl.BlockSpec(memory_space=pltpu.SMEM)] + [vmem] * 3,
        out_specs=[vmem] * 2,
        out_shape=[
            jax.ShapeDtypeStruct((width, width), jnp.float32),
            jax.ShapeDtypeStruct((width, width), jnp.float32),
        ],
        compiler_params=params(32),
        cost_estimate=pl.CostEstimate(
            flops=2 * 2 * rows * width * width, bytes_accessed=2 * MIB, transcendentals=0
        ),
        name="weight_parts",
    )(core.reshape(1), features, agg, grad)


def ring_sum(own, below, above, across, odd):
    own, below, above, across = (v.astype(jnp.float32) for v in (own, below, above, across))
    beside, beyond = jnp.where(odd, below, above), jnp.where(odd, above, below)
    return (own + beside) + (beyond + across)


def join_kernel(here_ref, below_ref, above_ref, *outs):
    rows = outs[0].shape[0]
    for k, out in enumerate(outs):
        part = slice(k * rows, (k + 1) * rows)
        out[...] = (
            here_ref[part, :].astype(jnp.float32)
            + below_ref[part, :].astype(jnp.float32)
            + above_ref[part, :].astype(jnp.float32)
        ).astype(jnp.bfloat16)


def join(here, below, above):
    total, width = here.shape
    vmem = pl.BlockSpec(memory_space=pltpu.VMEM)
    return pl.pallas_call(
        join_kernel,
        in_specs=[vmem] * 3,
        out_specs=[vmem] * 4,
        out_shape=[jax.ShapeDtypeStruct((total // 4, width), jnp.bfloat16)] * 4,
        compiler_params=params(32),
        cost_estimate=pl.CostEstimate(flops=0, bytes_accessed=4 * MIB, transcendentals=0),
        name="join",
    )(here, below, above)


def back_kernel(after_ref, grad_ref, self_ref, out_ref):
    cols_both = (((1,), (1,)), ((), ()))
    out_ref[...] = lax.dot_general(
        grad_ref[...], self_ref[...], cols_both, preferred_element_type=jnp.float32
    )


def self_back(after, grad, self_weight):
    vmem = pl.BlockSpec(memory_space=pltpu.VMEM)
    return pl.pallas_call(
        back_kernel,
        in_specs=[pl.BlockSpec(memory_space=pl.ANY), vmem, vmem],
        out_specs=vmem,
        out_shape=jax.ShapeDtypeStruct(grad.shape, jnp.float32),
        compiler_params=params(32),
        cost_estimate=pl.CostEstimate(flops=0, bytes_accessed=MIB, transcendentals=0),
        name="self_back",
    )(after, grad, self_weight)


def last_join_kernel(
    odd_ref, here_ref, below_ref, above_ref, back_ref, low_ref, weight_ref, sides_ref,
    rest_ref, down_ref, up_ref, across_ref, sum_ref,
):
    f32 = jnp.float32
    rows, total, count = back_ref.shape[0], here_ref.shape[0], weight_ref.shape[0]
    weight = ring_sum(
        weight_ref[...], sides_ref[:count, :], sides_ref[count:, :], below_ref[total:, :], odd_ref[0] == 1
    ).astype(jnp.bfloat16)
    sum_ref[...] = weight
    for k, out in enumerate((rest_ref, down_ref, up_ref, across_ref)):
        part = slice(k * rows, (k + 1) * rows)
        value = here_ref[part, :].astype(f32) + below_ref[part, :].astype(f32) + above_ref[part, :].astype(f32)
        if k == 0:
            out[...] = value + back_ref[...]
            continue
        if k == 3:
            value = value + low_ref[...].astype(f32)
        out[:rows, :] = value.astype(jnp.bfloat16)
        out[rows:, :] = weight


def last_join(odd, here, below, above, back, low, weight, weight_sides):
    rows, width = back.shape
    vmem = pl.BlockSpec(memory_space=pltpu.VMEM)
    message = jax.ShapeDtypeStruct((rows + weight.shape[0], width), jnp.bfloat16)
    return pl.pallas_call(
        last_join_kernel,
        in_specs=[pl.BlockSpec(memory_space=pltpu.SMEM)] + [vmem] * 7,
        out_specs=[vmem] * 5,
        out_shape=[
            jax.ShapeDtypeStruct((rows, width), jnp.float32),
            message, message, message,
            jax.ShapeDtypeStruct(weight.shape, jnp.bfloat16),
        ],
        compiler_params=params(32),
        cost_estimate=pl.CostEstimate(flops=0, bytes_accessed=6 * MIB, transcendentals=0),
        name="last_join",
    )(odd, here, below, above, back, low, weight, weight_sides)


def finish_kernel(norm, odd_ref, rest_ref, low_ref, down_ref, up_ref, across_ref, weight_ref, out_ref, sum_ref):
    rows = rest_ref.shape[0]
    arrived = (down_ref, up_ref, across_ref)
    total = rest_ref[...] + low_ref[...].astype(jnp.float32)
    for ref in arrived:
        total += ref[:rows, :].astype(jnp.float32)
    out_ref[...] = total.astype(jnp.bfloat16)
    above, below, across = (ref[rows:, :] for ref in arrived)
    sum_ref[...] = ring_sum(weight_ref[...], below, above, across, odd_ref[0] == 1) * norm


def finish(norm, odd, rest, low, from_above, from_below, from_across, weight):
    vmem = pl.BlockSpec(memory_space=pltpu.VMEM)
    return pl.pallas_call(
        functools.partial(finish_kernel, norm),
        in_specs=[pl.BlockSpec(memory_space=pltpu.SMEM)] + [vmem] * 6,
        out_specs=[vmem] * 2,
        out_shape=[
            jax.ShapeDtypeStruct(rest.shape, jnp.bfloat16),
            jax.ShapeDtypeStruct(weight.shape, jnp.float32),
        ],
        compiler_params=params(32),
        cost_estimate=pl.CostEstimate(flops=0, bytes_accessed=3 * MIB, transcendentals=0),
        name="finish",
    )(odd, rest, low, from_above, from_below, from_across, weight)


def plan_tiles(tile_rows, tile_cols, tile_sums, row_blocks):
    slots = tile_rows.shape[0]
    row_index, rep_index = lax.axis_index("row"), lax.axis_index("rep")
    z, x, y = row_index // 16, row_index // 4 % 4, row_index % 4
    core, high = rep_index % 2, rep_index // 2
    section, t = tile_cols // 16, tile_cols % 4
    far_z = (section // 16 != z).astype(jnp.int32)
    dx, dy = (section // 4 % 4 - x) % 4, (section % 4 - y) % 4
    dp, dq = jnp.where(core == 0, dx, dy), jnp.where(core == 0, dy, dx)
    kind = jnp.where(dq == 0, 0, 2 * far_z + jnp.where(dq == 2, 2, 1))
    kind = jnp.where(jnp.max(tile_sums, axis=1) > 0, kind, CLASSES)
    piece = jnp.where(dq == 0, far_z, (dq == 1).astype(jnp.int32))
    place = jnp.where(dp == 0, 0, jnp.where(dp == 3, 1, jnp.where(dp == 1, 2, 3)))
    block = piece * 16 + place * 4 + t
    slot = jnp.arange(slots, dtype=jnp.int32)
    code = slot + tile_rows * 1024 + block * 32768
    classes = jnp.arange(CLASSES, dtype=jnp.int32)
    counts = jnp.sum((kind[:, None] == classes[None, :]).astype(jnp.int32), axis=0)
    groups = (counts + GROUP - 1) // GROUP
    starts = jnp.sum(
        jnp.where(jnp.arange(CLASSES + 1)[:, None] > classes[None, :], groups[None, :], 0), axis=1
    )
    same_before = (kind[:, None] == kind[None, :]) & (slot[None, :] < slot[:, None])
    rank = jnp.sum(same_before.astype(jnp.int32), axis=1)
    start = jnp.sum(jnp.where(kind[:, None] == classes[None, :], starts[None, :CLASSES], 0), axis=1)
    position = jnp.where(kind < CLASSES, start * GROUP + rank, -1)
    places = -(-(slots + CLASSES * (GROUP - 1)) // GROUP) * GROUP
    hit = jnp.arange(places, dtype=jnp.int32)[:, None] == position[None, :]
    pad = row_blocks * 1024 + CLASS_BLOCKS * 32768
    meta = pad + jnp.sum(jnp.where(hit, code[None, :] - pad, 0), axis=1)
    bounds = jnp.concatenate([starts, core[None], high[None]]).astype(jnp.int32)
    return meta.astype(jnp.int32), bounds


def tie(*values):
    return lax.optimization_barrier(values)


def add(*values):
    return sum(value.astype(jnp.float32) for value in values).astype(jnp.bfloat16)


def local(features, self_weight, neigh_weight, tile_rows, tile_cols, tile_masks, cotangent):
    rows, width = features.shape
    row_blocks = rows * 4 // TILE
    core, high = lax.axis_index("rep") % 2, lax.axis_index("rep") // 2

    low = swap_low(features)
    near = [move_p(features, 1), move_p(features, -1), move_p(features, 2)]
    sums0, degree0 = degrees(0, 2, tile_rows, tile_masks, row_blocks)
    *near, low, sums0, degree0 = tie(*near, low, sums0, degree0)
    block0 = jnp.concatenate([features, *near])
    block0, far, low, rows_after = tie(block0, near[2], low, tile_rows)
    below0, above0 = move_q(block0, 1), move_q(block0, -1)
    near = [move_p(low, 1), move_p(low, -1), swap_low(far)]
    sums1, degree1 = degrees(1, 2, rows_after, tile_masks, row_blocks)
    *near, sums1, degree1 = tie(*near, sums1, degree1)
    block1 = jnp.concatenate([low, *near])
    block1, sums1 = tie(block1, sums1)
    below1, above1 = move_q(block1, 1), move_q(block1, -1)
    meta, bounds = plan_tiles(
        tile_rows, tile_cols, jnp.concatenate([sums0, sums1]), row_blocks
    )
    degree = degree0 + degree1
    degree = degree + swap_core(degree)

    def forward(begin, end, before, *pieces):
        return forward_class(begin, end, meta, bounds, tile_masks, pieces, before, row_blocks)

    total = forward(0, 1, None, block0, block1)
    below0, above0, total = tie(below0, above0, total)
    edge = block0.shape[0] // 2
    start0, start1 = below0[:edge], above0[edge:]
    start0, start1, total = tie(start0, start1, total)
    far00, far01 = move_q(start0, 1), move_q(start1, -1)
    total = forward(1, 2, total, below0, above0)
    below1, above1, total = tie(below1, above1, total)
    start0, start1 = below1[:edge], above1[edge:]
    start0, start1, total = tie(start0, start1, total)
    far10, far11 = move_q(start0, 1), move_q(start1, -1)
    total = forward(3, 4, total, below1, above1)
    far00, far01, total = tie(far00, far01, total)
    total = forward(2, 3, total, far00, far01)
    far10, far11, total = tie(far10, far11, total)
    keep, give = forward(4, 5, total, far10, far11)
    degree = degree + swap_high(degree)
    own_degree = lax.dynamic_slice_in_dim(
        degree, (high * 2 + core) * (row_blocks // 4), row_blocks // 4, 0
    )

    near = swap_core(give)
    far = swap_high(add(keep[1], near[1]))
    pre, neigh_near, cot_near, kept = before_dense(
        features, self_weight, neigh_weight, cotangent, keep
    )
    mean, grad, agg, output = dense(pre, neigh_near, cot_near, own_degree, kept, near, far)

    mean_far = swap_high(mean)
    mean_near = swap_core(mean)
    grads = (mean, mean_far, mean_near, swap_core(mean_far))
    weight_mine, weight_theirs = weight_parts(core, features, agg, grad)
    weight = (weight_mine + swap_core(weight_theirs)).astype(jnp.bfloat16)
    weight = add(weight, swap_low(weight))
    weight = add(weight, swap_high(weight))
    row_index = lax.axis_index("row")
    odd_x, odd_y = row_index // 4 % 2 == 1, row_index % 2 == 1
    odd_p, odd_q = jnp.where(core == 0, odd_x, odd_y), jnp.where(core == 0, odd_y, odd_x)

    def backward(which, grads, *arrived):
        return backward_class(which, meta, bounds, tile_masks, grads, *arrived)

    far10, far11 = backward(4, grads)
    far10, far11, *grads = tie(far10, far11, *grads)
    below1, above1 = move_q(far10, 1), move_q(far11, -1)
    far00, far01 = backward(2, grads)
    far00, far01, *grads = tie(far00, far01, *grads)
    far00, far01 = jnp.concatenate([far00, weight]), jnp.concatenate([far01, weight])
    below0, above0 = move_q(far00, 1), move_q(far01, -1)
    down, up = backward(3, grads, below1, above1)
    from_below1, from_above1 = move_q(up, 1), move_q(down, -1)
    down, up, weight_sides = backward(1, grads, below0, above0)
    from_below0, from_above0 = move_q(up, 1), move_q(down, -1)
    here0, here1 = backward(0, grads)
    here0, here1, from_below1, from_above1 = tie(here0, here1, from_below1, from_above1)
    odd_q, odd_p = (v.astype(jnp.int32).reshape(1) for v in (odd_q, odd_p))
    parts = join(here1, from_below1, from_above1)
    moved = (move_p(parts[1], -1), move_p(parts[2], 1))
    low_far = swap_low(parts[3])
    back = self_back(parts[0], grad, self_weight)
    own_part, *moved, low_far = tie(parts[0], *moved, low_far)
    low_own = swap_low(add(own_part, *moved))
    low_far, from_below0, from_above0 = tie(low_far, from_below0, from_above0)
    rest, down, up, across, weight = last_join(
        odd_q, here0, from_below0, from_above0, back, low_far,
        weight, weight_sides,
    )
    from_above, from_below, from_across = move_p(down, -1), move_p(up, 1), move_p(across, 2)
    norm = (rows * lax.axis_size(BOTH)) ** (-0.5)
    grad_feat, weight = finish(
        norm, odd_p, rest, low_own, from_above, from_below, from_across, weight
    )
    weight_other = swap_core(weight)
    self_total = jnp.where(core == 0, weight, weight_other)
    neigh_total = jnp.where(core == 0, weight_other, weight)
    return (output, grad_feat, self_total, neigh_total)


def solution(mesh):
    in_specs = (
        P(BOTH, None),
        P(),
        P(),
        P(BOTH),
        P(BOTH),
        P(BOTH, None, None),
        P(BOTH, None),
    )
    out_specs = (P(BOTH, None), P(BOTH, None), P(), P())
    return jax.shard_map(local, mesh=mesh, in_specs=in_specs, out_specs=out_specs, check_vma=False)
```

```python
import functools

import jax
import jax.numpy as jnp
from jax import lax
from jax.experimental import pallas as pl
from jax.experimental.pallas import tpu as pltpu
from jax.sharding import PartitionSpec as P

TILE = 128
GROUP = 16
DEPTH = 4
CLASSES = 5
CLASS_BLOCKS = 32
BLOCK_TILES = 16
BOTH = ("row", "rep")
MIB = 1024 * 1024


def pairs(step):
    out = []
    for z in range(2):
        for x in range(4):
            for y in range(4):
                for h in range(2):
                    for c in range(2):
                        src = (z * 16 + x * 4 + y) * 4 + h * 2 + c
                        z2, x2, y2, h2, c2 = step(z, x, y, h, c)
                        dst = ((z2 % 2) * 16 + (x2 % 4) * 4 + y2 % 4) * 4 + (h2 % 2) * 2 + c2 % 2
                        out.append((src, dst))
    return out


def move(value, step):
    return lax.ppermute(value, BOTH, pairs(step))


def swap_core(value):
    return move(value, lambda z, x, y, h, c: (z, x, y, h, c + 1))


def swap_high(value):
    return move(value, lambda z, x, y, h, c: (z, x, y, h + 1, c))


def swap_low(value):
    return move(value, lambda z, x, y, h, c: (z + 1, x, y, h, c))


def move_p(value, by):
    return move(value, lambda z, x, y, h, c: (z, x + by, y, h, c) if c == 0 else (z, x, y + by, h, c))


def move_q(value, by):
    return move(value, lambda z, x, y, h, c: (z, x, y + by, h, c) if c == 0 else (z, x + by, y, h, c))


def params(mib):
    return pltpu.CompilerParams(vmem_limit_bytes=mib * MIB)


def degree_kernel(first, rows_ref, masks_ref, tiles_ref, degree_ref, sums, buf, sems):
    count = tiles_ref.shape[0] // BLOCK_TILES

    def fetch(group):
        source = masks_ref.at[pl.ds(first + group * BLOCK_TILES, BLOCK_TILES)]
        slot = lax.rem(group, DEPTH)
        return pltpu.make_async_copy(source, buf.at[slot], sems.at[slot])

    for group in range(DEPTH - 1):
        fetch(group).start()
    sums[...] = jnp.zeros_like(sums)

    def turn(group, carry):
        @pl.when(group + DEPTH - 1 < count)
        def _():
            fetch(group + DEPTH - 1).start()

        fetch(group).wait()
        slot = lax.rem(group, DEPTH)
        for k in range(BLOCK_TILES):
            mask = buf[slot, k].astype(jnp.float32)
            row = rows_ref[first + group * BLOCK_TILES + k]
            sums[row] += mask
            tiles_ref[pl.ds(group * BLOCK_TILES + k, 1), :] = jnp.sum(mask, axis=0, keepdims=True)
        return carry

    lax.fori_loop(0, count, turn, 0)
    for r in range(degree_ref.shape[0]):
        degree_ref[pl.ds(r, 1), :] = jnp.sum(sums[r].T, axis=0, keepdims=True)


def degrees(part, parts, tile_rows, tile_masks, block_count):
    slots = tile_masks.shape[0] // parts
    vmem = pl.BlockSpec(memory_space=pltpu.VMEM)
    return pl.pallas_call(
        functools.partial(degree_kernel, part * slots),
        in_specs=[pl.BlockSpec(memory_space=pltpu.SMEM), pl.BlockSpec(memory_space=pltpu.HBM)],
        out_specs=[vmem, vmem],
        out_shape=[
            jax.ShapeDtypeStruct((slots, TILE), jnp.float32),
            jax.ShapeDtypeStruct((block_count, TILE), jnp.float32),
        ],
        scratch_shapes=[
            pltpu.VMEM((block_count, TILE, TILE), jnp.float32),
            pltpu.VMEM((DEPTH, BLOCK_TILES, TILE, TILE), jnp.int32),
            pltpu.SemaphoreType.DMA((DEPTH,)),
        ],
        compiler_params=params(41),
        cost_estimate=pl.CostEstimate(flops=0, bytes_accessed=20 * MIB, transcendentals=0),
        name=f"degrees{part}",
    )(tile_rows, tile_masks)


def unpack(meta):
    return meta & 1023, (meta >> 10) & 31, meta >> 15


def as_bf16(mask):
    return mask.astype(jnp.float32).astype(jnp.bfloat16)


def fetch_tiles(group, meta_ref, masks_ref, buf, sems):
    slot = lax.rem(group, DEPTH)
    for u in range(GROUP):
        tile = unpack(meta_ref[group * GROUP + u])[0]
        pltpu.make_async_copy(masks_ref.at[tile], buf.at[slot, u], sems.at[slot]).start()


def first_groups(first, last, *fetch_args):
    for ahead in range(DEPTH - 1):

        @pl.when(first + ahead < last)
        def _():
            fetch_tiles(first + ahead, *fetch_args)


def each_group(first, last, meta_ref, masks_ref, buf, sems, body):
    def turn(group, carry):
        @pl.when(group + DEPTH - 1 < last)
        def _():
            fetch_tiles(group + DEPTH - 1, meta_ref, masks_ref, buf, sems)

        slot = lax.rem(group, DEPTH)
        pltpu.make_async_copy(masks_ref.at[pl.ds(0, GROUP)], buf.at[slot], sems.at[slot]).wait()
        body(group, slot)
        return carry

    lax.fori_loop(first, last, turn, 0)


def forward_kernel(begin, end, count, first_call, last_call, meta_ref, bounds_ref, masks_ref, *refs):
    pieces = refs[:count]
    refs = refs[count:]
    before = None
    if not first_call:
        before, refs = refs[0], refs[1:]
    if last_call:
        keep_ref, give_ref, feats, buf, sems, total = refs
    else:
        total, feats, buf, sems = refs
    first, last = bounds_ref[begin], bounds_ref[end]
    first_groups(first, last, meta_ref, masks_ref, buf, sems)
    start = 0
    for piece in pieces:
        feats[start : start + piece.shape[0], :] = piece[...]
        start += piece.shape[0]
    total[...] = jnp.zeros_like(total) if first_call else before[...]

    def body(group, slot):
        for u in range(GROUP):
            _, row, block = unpack(meta_ref[group * GROUP + u])
            part = jnp.dot(
                as_bf16(buf[slot, u]),
                feats[pl.ds(pl.multiple_of(block * TILE, TILE), TILE), :],
                preferred_element_type=jnp.float32,
            )
            total[pl.ds(pl.multiple_of(row * TILE, TILE), TILE), :] += part

    each_group(first, last, meta_ref, masks_ref, buf, sems, body)
    if last_call:
        quarter = keep_ref.shape[1]
        core, high = bounds_ref[CLASSES + 1], bounds_ref[CLASSES + 2]
        for h in range(2):
            side = (high + h) % 2
            kept = pl.multiple_of((side * 2 + core) * quarter, quarter)
            given = pl.multiple_of((side * 2 + 1 - core) * quarter, quarter)
            keep_ref[h] = total[pl.ds(kept, quarter), :].astype(jnp.bfloat16)
            give_ref[h] = total[pl.ds(given, quarter), :].astype(jnp.bfloat16)


def forward_class(begin, end, meta, bounds, masks, pieces, before, row_blocks):
    width = pieces[0].shape[-1]
    first_call, last_call = before is None, end == CLASSES

    total_rows = (row_blocks + 1) * TILE
    feat_rows = (CLASS_BLOCKS + 1) * TILE
    scratch = [
        pltpu.VMEM((feat_rows, width), jnp.bfloat16),
        pltpu.VMEM((DEPTH, GROUP, TILE, TILE), jnp.int32),
        pltpu.SemaphoreType.DMA((DEPTH,)),
    ]
    vmem = pl.BlockSpec(memory_space=pltpu.VMEM)
    if last_call:
        half = jax.ShapeDtypeStruct((2, row_blocks * TILE // 4, width), jnp.bfloat16)
        out_shape, out_specs = [half, half], [vmem, vmem]
        scratch.append(pltpu.VMEM((total_rows, width), jnp.float32))
    else:
        out_shape, out_specs = jax.ShapeDtypeStruct((total_rows, width), jnp.float32), vmem
    smem = pl.BlockSpec(memory_space=pltpu.SMEM)
    held = pl.BlockSpec(memory_space=pltpu.HBM)
    extra = [] if first_call else [before]
    aliases = {} if first_call or last_call else {3 + len(pieces): 0}
    return pl.pallas_call(
        functools.partial(forward_kernel, begin, end, len(pieces), first_call, last_call),
        in_specs=[smem, smem, held] + [vmem] * (len(pieces) + len(extra)),
        out_specs=out_specs,
        out_shape=out_shape,
        scratch_shapes=scratch,
        input_output_aliases=aliases,
        compiler_params=params(41),
        cost_estimate=pl.CostEstimate(flops=0, bytes_accessed=16 * MIB, transcendentals=0),
        name=f"forward_class{begin}",
    )(meta, bounds, masks, *pieces, *extra)


def backward_kernel(which, count, meta_ref, bounds_ref, masks_ref, own, far, near, cross, *refs):
    arrived, refs = (refs[:2], refs[2:]) if which % 2 else (None, refs)
    if which == 4:
        weight, refs = refs[0], refs[1:]
    outs, refs = refs[:count], refs[count:]
    if which in (1, 4):
        passed, refs = refs[0], refs[1:]
    if which == 4:
        passed[...] = weight[...]
    grads, buf, sems, total = refs
    quarter = own.shape[0]
    core, high = bounds_ref[CLASSES + 1], bounds_ref[CLASSES + 2]
    first, last = bounds_ref[which], bounds_ref[which + 1]
    first_groups(first, last, meta_ref, masks_ref, buf, sems)
    for piece, h, c in ((own, 0, 0), (far, 1, 0), (near, 0, 1), (cross, 1, 1)):
        place = ((high + h) % 2) * 2 + (core + c) % 2
        grads[pl.ds(pl.multiple_of(place * quarter, quarter), quarter), :] = piece[...]
    if arrived is None:
        total[...] = jnp.zeros_like(total)
    else:
        below, above = arrived
        edge = CLASS_BLOCKS * TILE // 4
        total[:edge, :] = jnp.zeros((edge, total.shape[1]), jnp.float32)
        total[edge : 2 * edge, :] = above[:edge, :].astype(jnp.float32)
        total[2 * edge : 3 * edge, :] = below[:edge, :].astype(jnp.float32)
        total[3 * edge :, :] = jnp.zeros((edge + TILE, total.shape[1]), jnp.float32)

    def body(group, slot):
        for u in range(GROUP):
            _, row, block = unpack(meta_ref[group * GROUP + u])
            part = lax.dot_general(
                as_bf16(buf[slot, u]),
                grads[pl.ds(pl.multiple_of(row * TILE, TILE), TILE), :],
                (((0,), (0,)), ((), ())),
                preferred_element_type=jnp.float32,
            )
            total[pl.ds(pl.multiple_of(block * TILE, TILE), TILE), :] += part

    each_group(first, last, meta_ref, masks_ref, buf, sems, body)
    size = CLASS_BLOCKS * TILE // (2 if which in (0, 1, 3) else 4)
    for k, out in enumerate(outs):
        out[:size, :] = total[k * size : (k + 1) * size, :].astype(jnp.bfloat16)
    if which == 1:
        behind = below.shape[0] - edge
        outs[1][size:, :] = below[edge:, :]
        passed[:behind, :] = below[edge:, :]
        passed[behind:, :] = above[edge:, :]


def backward_class(which, meta, bounds, masks, grads, *arrived):
    quarter, width = grads[0].shape
    vmem = pl.BlockSpec(memory_space=pltpu.VMEM)
    smem = pl.BlockSpec(memory_space=pltpu.SMEM)
    held = pl.BlockSpec(memory_space=pltpu.HBM)
    count = 2
    blocks = CLASS_BLOCKS // 2 if which in (2, 4) else CLASS_BLOCKS
    sizes = [blocks * TILE // count] * count
    if which == 1:
        behind = arrived[0].shape[0] - sizes[0] // 2
        sizes = [sizes[0], sizes[1] + behind, 2 * behind]
    if which == 4:
        sizes.append(arrived[0].shape[0])
    return pl.pallas_call(
        functools.partial(backward_kernel, which, count),
        in_specs=[smem, smem, held] + [vmem] * (4 + len(arrived)),
        out_specs=[vmem] * len(sizes),
        out_shape=[jax.ShapeDtypeStruct((size, width), jnp.bfloat16) for size in sizes],
        scratch_shapes=[
            pltpu.VMEM((4 * quarter + TILE, width), jnp.bfloat16),
            pltpu.VMEM((DEPTH, GROUP, TILE, TILE), jnp.int32),
            pltpu.SemaphoreType.DMA((DEPTH,)),
            pltpu.VMEM(((CLASS_BLOCKS + 1) * TILE, width), jnp.float32),
        ],
        compiler_params=params(41),
        cost_estimate=pl.CostEstimate(flops=0, bytes_accessed=16 * MIB, transcendentals=0),
        name=f"backward_class{which}",
    )(meta, bounds, masks, *grads, *arrived)


def before_kernel(feat_ref, self_ref, neigh_ref, cot_ref, keep_ref, pre_ref, neigh_out, cot_out, sum_ref):
    pre_ref[...] = jnp.dot(feat_ref[...], self_ref[...], preferred_element_type=jnp.float32)
    neigh_out[...] = neigh_ref[...]
    cot_out[...] = cot_ref[...]
    sum_ref[...] = keep_ref[0]


def before_dense(features, self_weight, neigh_weight, cotangent, keep):
    rows, width = features.shape
    vmem = pl.BlockSpec(memory_space=pltpu.VMEM)
    return pl.pallas_call(
        before_kernel,
        in_specs=[vmem] * 5,
        out_specs=[vmem] * 4,
        out_shape=[
            jax.ShapeDtypeStruct((rows, width), jnp.float32),
            jax.ShapeDtypeStruct((width, width), jnp.bfloat16),
            jax.ShapeDtypeStruct((rows, width), jnp.bfloat16),
            jax.ShapeDtypeStruct((rows, width), jnp.bfloat16),
        ],
        compiler_params=params(16),
        cost_estimate=pl.CostEstimate(
            flops=2 * rows * width * width, bytes_accessed=2 * MIB, transcendentals=0
        ),
        name="before_dense",
    )(features, self_weight, neigh_weight, cotangent, keep)


def dense_kernel(
    pre_ref, neigh_ref, cot_ref, degree_ref, keep_ref, near_ref, far_ref,
    mean_ref, grad_ref, agg_ref, out_ref,
):
    cols_both = (((1,), (1,)), ((), ()))
    f32 = jnp.float32
    inverse = lax.rsqrt(jnp.maximum(degree_ref[...], 1.0))
    width = pre_ref.shape[1]
    columns = [
        jnp.broadcast_to(inverse[r : r + 1, :], (TILE, TILE)).T for r in range(inverse.shape[0])
    ]
    scale = jnp.concatenate([jnp.concatenate(columns, axis=0)] * (width // TILE), axis=1)
    summed = keep_ref[...].astype(f32) + near_ref[0].astype(f32) + far_ref[...].astype(f32)
    agg = (summed * scale).astype(jnp.bfloat16)
    pre = pre_ref[...] + jnp.dot(agg, neigh_ref[...], preferred_element_type=f32)
    sig = jax.nn.sigmoid(pre)
    out_ref[...] = (pre * sig).astype(jnp.bfloat16)
    grad = (cot_ref[...].astype(f32) * sig * (1.0 + pre * (1.0 - sig))).astype(jnp.bfloat16)
    mean = lax.dot_general(grad, neigh_ref[...], cols_both, preferred_element_type=f32) * scale
    mean_ref[...] = mean.astype(jnp.bfloat16)
    grad_ref[...] = grad
    agg_ref[...] = agg


def dense(pre, neigh_weight, cotangent, degree, keep, near, far):
    rows, width = pre.shape
    vmem = pl.BlockSpec(memory_space=pltpu.VMEM)
    return pl.pallas_call(
        dense_kernel,
        in_specs=[vmem] * 7,
        out_specs=[vmem] * 4,
        out_shape=[jax.ShapeDtypeStruct((rows, width), jnp.bfloat16)] * 4,
        compiler_params=params(16),
        cost_estimate=pl.CostEstimate(
            flops=2 * 2 * rows * width * width, bytes_accessed=4 * MIB, transcendentals=rows * width
        ),
        name="dense",
    )(pre, neigh_weight, cotangent, degree, keep, near, far)


def weights_kernel(core_ref, feat_ref, agg_ref, grad_ref, mine_ref, theirs_ref):
    rows_first = (((0,), (0,)), ((), ()))
    f32 = jnp.float32
    grad = grad_ref[...]
    parts = [
        lax.dot_general(value[...], grad, rows_first, preferred_element_type=f32)
        for value in (feat_ref, agg_ref)
    ]
    on_first = core_ref[0] == 0
    mine_ref[...] = jnp.where(on_first, parts[0], parts[1])
    theirs_ref[...] = jnp.where(on_first, parts[1], parts[0])


def weight_parts(core, features, agg, grad):
    rows, width = features.shape
    vmem = pl.BlockSpec(memory_space=pltpu.VMEM)
    return pl.pallas_call(
        weights_kernel,
        in_specs=[pl.BlockSpec(memory_space=pltpu.SMEM)] + [vmem] * 3,
        out_specs=[vmem] * 2,
        out_shape=[
            jax.ShapeDtypeStruct((width, width), jnp.float32),
            jax.ShapeDtypeStruct((width, width), jnp.float32),
        ],
        compiler_params=params(16),
        cost_estimate=pl.CostEstimate(
            flops=2 * 2 * rows * width * width, bytes_accessed=2 * MIB, transcendentals=0
        ),
        name="weight_parts",
    )(core.reshape(1), features, agg, grad)


def ring_sum(own, below, above, across, odd):
    own, below, above, across = (v.astype(jnp.float32) for v in (own, below, above, across))
    beside, beyond = jnp.where(odd, below, above), jnp.where(odd, above, below)
    return (own + beside) + (beyond + across)


def join_kernel(here_ref, below_ref, above_ref, *outs):
    rows = outs[0].shape[0]
    for k, out in enumerate(outs):
        part = slice(k * rows, (k + 1) * rows)
        out[...] = (
            here_ref[part, :].astype(jnp.float32)
            + below_ref[part, :].astype(jnp.float32)
            + above_ref[part, :].astype(jnp.float32)
        ).astype(jnp.bfloat16)


def join(here, below, above):
    total, width = here.shape
    vmem = pl.BlockSpec(memory_space=pltpu.VMEM)
    return pl.pallas_call(
        join_kernel,
        in_specs=[vmem] * 3,
        out_specs=[vmem] * 4,
        out_shape=[jax.ShapeDtypeStruct((total // 4, width), jnp.bfloat16)] * 4,
        compiler_params=params(16),
        cost_estimate=pl.CostEstimate(flops=0, bytes_accessed=4 * MIB, transcendentals=0),
        name="join",
    )(here, below, above)


def back_kernel(after_ref, grad_ref, self_ref, out_ref):
    cols_both = (((1,), (1,)), ((), ()))
    out_ref[...] = lax.dot_general(
        grad_ref[...], self_ref[...], cols_both, preferred_element_type=jnp.float32
    )


def self_back(after, grad, self_weight):
    vmem = pl.BlockSpec(memory_space=pltpu.VMEM)
    return pl.pallas_call(
        back_kernel,
        in_specs=[pl.BlockSpec(memory_space=pl.ANY), vmem, vmem],
        out_specs=vmem,
        out_shape=jax.ShapeDtypeStruct(grad.shape, jnp.float32),
        compiler_params=params(16),
        cost_estimate=pl.CostEstimate(flops=0, bytes_accessed=MIB, transcendentals=0),
        name="self_back",
    )(after, grad, self_weight)


def last_join_kernel(
    odd_ref, here_ref, below_ref, above_ref, back_ref, low_ref, weight_ref, sides_ref,
    rest_ref, down_ref, up_ref, across_ref, sum_ref,
):
    f32 = jnp.float32
    rows, total, count = back_ref.shape[0], here_ref.shape[0], weight_ref.shape[0]
    weight = ring_sum(
        weight_ref[...], sides_ref[:count, :], sides_ref[count:, :], below_ref[total:, :], odd_ref[0] == 1
    ).astype(jnp.bfloat16)
    sum_ref[...] = weight
    for k, out in enumerate((rest_ref, down_ref, up_ref, across_ref)):
        part = slice(k * rows, (k + 1) * rows)
        value = here_ref[part, :].astype(f32) + below_ref[part, :].astype(f32) + above_ref[part, :].astype(f32)
        if k == 0:
            out[...] = value + back_ref[...]
            continue
        if k == 3:
            value = value + low_ref[...].astype(f32)
        out[:rows, :] = value.astype(jnp.bfloat16)
        out[rows:, :] = weight


def last_join(odd, here, below, above, back, low, weight, weight_sides):
    rows, width = back.shape
    vmem = pl.BlockSpec(memory_space=pltpu.VMEM)
    message = jax.ShapeDtypeStruct((rows + weight.shape[0], width), jnp.bfloat16)
    return pl.pallas_call(
        last_join_kernel,
        in_specs=[pl.BlockSpec(memory_space=pltpu.SMEM)] + [vmem] * 7,
        out_specs=[vmem] * 5,
        out_shape=[
            jax.ShapeDtypeStruct((rows, width), jnp.float32),
            message, message, message,
            jax.ShapeDtypeStruct(weight.shape, jnp.bfloat16),
        ],
        compiler_params=params(16),
        cost_estimate=pl.CostEstimate(flops=0, bytes_accessed=6 * MIB, transcendentals=0),
        name="last_join",
    )(odd, here, below, above, back, low, weight, weight_sides)


def finish_kernel(norm, odd_ref, rest_ref, low_ref, down_ref, up_ref, across_ref, weight_ref, out_ref, sum_ref):
    rows = rest_ref.shape[0]
    arrived = (down_ref, up_ref, across_ref)
    total = rest_ref[...] + low_ref[...].astype(jnp.float32)
    for ref in arrived:
        total += ref[:rows, :].astype(jnp.float32)
    out_ref[...] = total.astype(jnp.bfloat16)
    above, below, across = (ref[rows:, :] for ref in arrived)
    sum_ref[...] = ring_sum(weight_ref[...], below, above, across, odd_ref[0] == 1) * norm


def finish(norm, odd, rest, low, from_above, from_below, from_across, weight):
    vmem = pl.BlockSpec(memory_space=pltpu.VMEM)
    return pl.pallas_call(
        functools.partial(finish_kernel, norm),
        in_specs=[pl.BlockSpec(memory_space=pltpu.SMEM)] + [vmem] * 6,
        out_specs=[vmem] * 2,
        out_shape=[
            jax.ShapeDtypeStruct(rest.shape, jnp.bfloat16),
            jax.ShapeDtypeStruct(weight.shape, jnp.float32),
        ],
        compiler_params=params(16),
        cost_estimate=pl.CostEstimate(flops=0, bytes_accessed=3 * MIB, transcendentals=0),
        name="finish",
    )(odd, rest, low, from_above, from_below, from_across, weight)


def plan_tiles(tile_rows, tile_cols, tile_sums, row_blocks):
    slots = tile_rows.shape[0]
    row_index, rep_index = lax.axis_index("row"), lax.axis_index("rep")
    z, x, y = row_index // 16, row_index // 4 % 4, row_index % 4
    core, high = rep_index % 2, rep_index // 2
    section, t = tile_cols // 16, tile_cols % 4
    far_z = (section // 16 != z).astype(jnp.int32)
    dx, dy = (section // 4 % 4 - x) % 4, (section % 4 - y) % 4
    dp, dq = jnp.where(core == 0, dx, dy), jnp.where(core == 0, dy, dx)
    kind = jnp.where(dq == 0, 0, 2 * far_z + jnp.where(dq == 2, 2, 1))
    kind = jnp.where(jnp.max(tile_sums, axis=1) > 0, kind, CLASSES)
    piece = jnp.where(dq == 0, far_z, (dq == 1).astype(jnp.int32))
    place = jnp.where(dp == 0, 0, jnp.where(dp == 3, 1, jnp.where(dp == 1, 2, 3)))
    block = piece * 16 + place * 4 + t
    slot = jnp.arange(slots, dtype=jnp.int32)
    code = slot + tile_rows * 1024 + block * 32768
    classes = jnp.arange(CLASSES, dtype=jnp.int32)
    counts = jnp.sum((kind[:, None] == classes[None, :]).astype(jnp.int32), axis=0)
    groups = (counts + GROUP - 1) // GROUP
    starts = jnp.sum(
        jnp.where(jnp.arange(CLASSES + 1)[:, None] > classes[None, :], groups[None, :], 0), axis=1
    )
    same_before = (kind[:, None] == kind[None, :]) & (slot[None, :] < slot[:, None])
    rank = jnp.sum(same_before.astype(jnp.int32), axis=1)
    start = jnp.sum(jnp.where(kind[:, None] == classes[None, :], starts[None, :CLASSES], 0), axis=1)
    position = jnp.where(kind < CLASSES, start * GROUP + rank, -1)
    places = -(-(slots + CLASSES * (GROUP - 1)) // GROUP) * GROUP
    hit = jnp.arange(places, dtype=jnp.int32)[:, None] == position[None, :]
    pad = row_blocks * 1024 + CLASS_BLOCKS * 32768
    meta = pad + jnp.sum(jnp.where(hit, code[None, :] - pad, 0), axis=1)
    bounds = jnp.concatenate([starts, core[None], high[None]]).astype(jnp.int32)
    return meta.astype(jnp.int32), bounds


def tie(*values):
    return lax.optimization_barrier(values)


def add(*values):
    return sum(value.astype(jnp.float32) for value in values).astype(jnp.bfloat16)


def local(features, self_weight, neigh_weight, tile_rows, tile_cols, tile_masks, cotangent):
    rows, width = features.shape
    row_blocks = rows * 4 // TILE
    core, high = lax.axis_index("rep") % 2, lax.axis_index("rep") // 2

    low = swap_low(features)
    near = [move_p(features, 1), move_p(features, -1), move_p(features, 2)]
    sums0, degree0 = degrees(0, 2, tile_rows, tile_masks, row_blocks)
    *near, low, sums0, degree0 = tie(*near, low, sums0, degree0)
    block0 = jnp.concatenate([features, *near])
    block0, far, low, rows_after = tie(block0, near[2], low, tile_rows)
    below0, above0 = move_q(block0, 1), move_q(block0, -1)
    near = [move_p(low, 1), move_p(low, -1), swap_low(far)]
    sums1, degree1 = degrees(1, 2, rows_after, tile_masks, row_blocks)
    *near, sums1, degree1 = tie(*near, sums1, degree1)
    block1 = jnp.concatenate([low, *near])
    block1, sums1 = tie(block1, sums1)
    below1, above1 = move_q(block1, 1), move_q(block1, -1)
    meta, bounds = plan_tiles(
        tile_rows, tile_cols, jnp.concatenate([sums0, sums1]), row_blocks
    )
    degree = degree0 + degree1
    degree = degree + swap_core(degree)

    def forward(begin, end, before, *pieces):
        return forward_class(begin, end, meta, bounds, tile_masks, pieces, before, row_blocks)

    total = forward(0, 1, None, block0, block1)
    below0, above0, total = tie(below0, above0, total)
    edge = block0.shape[0] // 2
    start0, start1 = below0[:edge], above0[edge:]
    start0, start1, total = tie(start0, start1, total)
    far00, far01 = move_q(start0, 1), move_q(start1, -1)
    total = forward(1, 2, total, below0, above0)
    below1, above1, total = tie(below1, above1, total)
    start0, start1 = below1[:edge], above1[edge:]
    start0, start1, total = tie(start0, start1, total)
    far10, far11 = move_q(start0, 1), move_q(start1, -1)
    total = forward(3, 4, total, below1, above1)
    far00, far01, total = tie(far00, far01, total)
    total = forward(2, 3, total, far00, far01)
    far10, far11, total = tie(far10, far11, total)
    keep, give = forward(4, 5, total, far10, far11)
    degree = degree + swap_high(degree)
    own_degree = lax.dynamic_slice_in_dim(
        degree, (high * 2 + core) * (row_blocks // 4), row_blocks // 4, 0
    )

    near = swap_core(give)
    far = swap_high(add(keep[1], near[1]))
    pre, neigh_near, cot_near, kept = before_dense(
        features, self_weight, neigh_weight, cotangent, keep
    )
    mean, grad, agg, output = dense(pre, neigh_near, cot_near, own_degree, kept, near, far)

    mean_far = swap_high(mean)
    mean_near = swap_core(mean)
    grads = (mean, mean_far, mean_near, swap_core(mean_far))
    weight_mine, weight_theirs = weight_parts(core, features, agg, grad)
    weight = (weight_mine + swap_core(weight_theirs)).astype(jnp.bfloat16)
    weight_low = swap_low(weight)
    row_index = lax.axis_index("row")
    odd_x, odd_y = row_index // 4 % 2 == 1, row_index % 2 == 1
    odd_p, odd_q = jnp.where(core == 0, odd_x, odd_y), jnp.where(core == 0, odd_y, odd_x)

    def backward(which, grads, *arrived):
        return backward_class(which, meta, bounds, tile_masks, grads, *arrived)

    far10, far11, weight = backward(4, grads, weight)
    weight = add(weight, weight_low)
    weight = add(weight, swap_high(weight))
    far10, far11, *grads = tie(far10, far11, *grads)
    below1, above1 = move_q(far10, 1), move_q(far11, -1)
    far00, far01 = backward(2, grads)
    far00, far01, *grads = tie(far00, far01, *grads)
    far00, far01 = jnp.concatenate([far00, weight]), jnp.concatenate([far01, weight])
    below0, above0 = move_q(far00, 1), move_q(far01, -1)
    down, up = backward(3, grads, below1, above1)
    from_below1, from_above1 = move_q(up, 1), move_q(down, -1)
    down, up, weight_sides = backward(1, grads, below0, above0)
    from_below0, from_above0 = move_q(up, 1), move_q(down, -1)
    here0, here1 = backward(0, grads)
    here0, here1, from_below1, from_above1 = tie(here0, here1, from_below1, from_above1)
    odd_q, odd_p = (v.astype(jnp.int32).reshape(1) for v in (odd_q, odd_p))
    parts = join(here1, from_below1, from_above1)
    moved = (move_p(parts[1], -1), move_p(parts[2], 1))
    low_far = swap_low(parts[3])
    back = self_back(parts[0], grad, self_weight)
    own_part, *moved, low_far = tie(parts[0], *moved, low_far)
    low_own = swap_low(add(own_part, *moved))
    low_far, from_below0, from_above0 = tie(low_far, from_below0, from_above0)
    rest, down, up, across, weight = last_join(
        odd_q, here0, from_below0, from_above0, back, low_far,
        weight, weight_sides,
    )
    from_above, from_below, from_across = move_p(down, -1), move_p(up, 1), move_p(across, 2)
    norm = (rows * lax.axis_size(BOTH)) ** (-0.5)
    grad_feat, weight = finish(
        norm, odd_p, rest, low_own, from_above, from_below, from_across, weight
    )
    weight_other = swap_core(weight)
    self_total = jnp.where(core == 0, weight, weight_other)
    neigh_total = jnp.where(core == 0, weight_other, weight)
    return (output, grad_feat, self_total, neigh_total)


def solution(mesh):
    in_specs = (
        P(BOTH, None),
        P(),
        P(),
        P(BOTH),
        P(BOTH),
        P(BOTH, None, None),
        P(BOTH, None),
    )
    out_specs = (P(BOTH, None), P(BOTH, None), P(), P())
    return jax.shard_map(local, mesh=mesh, in_specs=in_specs, out_specs=out_specs, check_vma=False)
```
